128 devices in a mesh: dp: 8 (over z, core), list: 16 (over x, y).
Axes of the slice: x: 4, y: 4, z: 4, core: 2. Of those that a mesh axis runs over, the one named last changes fastest.
Arguments:
- candidates: bfloat16 [8, 2048, 1024], P('dp', 'list'), may hold values from -6 to 6
- counts: int32 [8], P('dp'), may hold values from 204 to 2048, as said below
- hist_keys: bfloat16 [8, 256, 1024], P('dp', 'list'), may hold values from -60 to 60
- hist_values: bfloat16 [8, 256, 1024], P('dp', 'list'), may hold values from -6 to 6
- hist_lengths: int32 [8], P('dp'), may hold values from 25 to 256, as said below
- gain: float32 [1024], replicated, may hold values from 0.5 to 1.5
- w_query: bfloat16 [1024, 1024], replicated, may hold values from -0.1875 to 0.1875
- w_key: bfloat16 [1024, 1024], replicated, may hold values from -0.1875 to 0.1875
- w_value: bfloat16 [1024, 1024], replicated, may hold values from -0.1875 to 0.1875
- cotangent: bfloat16 [8, 2048, 1024], P('dp', 'list'), may hold values from -6 to 6
Outputs:
- output: bfloat16 [8, 2048, 1024], P('dp', 'list')
- grad_x: bfloat16 [8, 2048, 1024], P('dp', 'list')
- grad_wq: float32 [1024, 1024], P(('dp', 'list'))
- grad_wk: float32 [1024, 1024], P(('dp', 'list'))
- grad_wv: float32 [1024, 1024], P(('dp', 'list'))
- grad_gain: float32 [1024], P(('dp', 'list'))
The draws below stay inside these ranges and needn't reach their ends.
Inputs may be any that keep to these rules, and one draw needn't show every extreme that they name: `counts`: one request in every draw has exactly 2048 live candidates, another the fewest. `hist_lengths`: one request in every draw has exactly 256 live history actions, another the fewest.
All inputs are finite; a program needn't handle non-finite values.
Results may differ from the reference program's by a relative error of at most 0.025.
The reference program's roundings to bfloat16 on the way (of `normed`, `mixed`, `grad_mix` and `grad_scores`) count: a program that leaves them out, or rounds other values in their place, can miss the bound.
Values may be sent and summed in bfloat16 or wider, within the bound.
No kernel may reach another device: no remote copies, remote signals or barrier semaphores. Data moves between devices by JAX's collectives and lax.ppermute only.
A program may use at most 192 MiB of HBM per device.

```python
import math
import jax
import jax.numpy as jnp
from jax import lax

D = 1024
H = 16
HEAD = 64
CAND = 2048
HIST = 256
REQUESTS = 8


def draw_counts(key, part):
    key = jax.random.fold_in(key, 3)
    drawn = jax.random.randint(key, (REQUESTS,), max(1, CAND // 10), CAND + 1)
    drawn = drawn.at[1].set(max(1, CAND // 10))
    return drawn.at[0].set(CAND).astype(jnp.int32)


def draw_hist_lengths(key, part):
    key = jax.random.fold_in(key, 5)
    drawn = jax.random.randint(key, (REQUESTS,), max(1, HIST // 10), HIST + 1)
    drawn = drawn.at[0].set(max(1, HIST // 10))
    return drawn.at[REQUESTS - 1].set(HIST).astype(jnp.int32)


def draw_hist_keys(key, part):
    key = jax.random.fold_in(key, 7)
    base = jnp.clip(jax.random.normal(key, (REQUESTS, HIST, D), jnp.float32), -6.0, 6.0)
    return base.astype(jnp.bfloat16)


def block_levels(rng, extent, split, smallest, largest):
    def one(position, blocks):
        steps = jax.random.uniform(jax.random.fold_in(jax.random.fold_in(rng, 6), position), (blocks,), jnp.float32, smallest / len(split), largest / len(split))
        return jnp.repeat(jnp.exp(steps), extent[position] // blocks).reshape((-1,) + (1,) * (len(extent) - position - 1))

    level = one(*split[0])
    for cut in split[1:]:
        level = level * one(*cut)
    return level


def centred(key, shape, scale, limit, split=(), held_as=jnp.bfloat16):
    entries = scale * jax.random.normal(key, shape, jnp.float32)
    if split:
        entries = entries * block_levels(key, shape, split, -0.22, 0.18)
    return jnp.clip(entries, -limit, limit).astype(held_as)


def setup_inputs(seed: int = 0) -> dict:
    key_of = jax.random.split(jax.random.key(seed), 11)
    return {
        "candidates": centred(key_of[0], (REQUESTS, CAND, D), 1.0, 6.0, ((0, 8), (1, 16))),
        "counts": draw_counts(jax.random.fold_in(key_of[10], 71), 0),
        "hist_keys": draw_hist_keys(jax.random.fold_in(key_of[10], 71), 0),
        "hist_values": centred(key_of[3], (REQUESTS, HIST, D), 1.0, 6.0, ((0, 8), (1, 16))),
        "hist_lengths": draw_hist_lengths(jax.random.fold_in(key_of[10], 71), 0),
        "gain": jnp.clip(1.0 + 0.1 * jax.random.normal(key_of[5], (D,), jnp.float32), 0.5, 1.5),
        "w_query": centred(key_of[6], (D, D), D ** -0.5, 0.1875),
        "w_key": centred(key_of[7], (D, D), D ** -0.5, 0.1875),
        "w_value": centred(key_of[8], (D, D), D ** -0.5, 0.1875),
        "cotangent": centred(key_of[9], (REQUESTS, CAND, D), 1.0, 6.0, ((0, 8), (1, 16))),
    }


negative_fill = -1e+30

def reference(candidates, counts, hist_keys, hist_values, hist_lengths, gain, w_query, w_key, w_value, cotangent):
    scale = 1.0 / math.sqrt(HEAD)
    gains = gain.astype(jnp.float32)

    def per_request(item):
        feats_in, count, hkeys, hvals, hlength, cot = item
        feats = feats_in.astype(jnp.float32)
        mean_sq = lax.optimization_barrier(jnp.mean(feats * feats, axis=-1, keepdims=True))
        inv_rms = lax.rsqrt(mean_sq + 1e-05)
        normed = (feats * inv_rms * gains).astype(jnp.bfloat16)
        query = jnp.dot(normed, w_query, preferred_element_type=jnp.float32).astype(jnp.bfloat16)
        key_rows = jnp.dot(normed, w_key, preferred_element_type=jnp.float32).astype(jnp.bfloat16)
        value_rows = jnp.dot(normed, w_value, preferred_element_type=jnp.float32).astype(jnp.bfloat16)
        all_keys = jnp.concatenate([hkeys, key_rows], 0)
        all_values = jnp.concatenate([hvals, value_rows], 0)
        heads_q = query.reshape(CAND, H, HEAD).astype(jnp.float32)
        heads_k = all_keys.reshape(HIST + CAND, H, HEAD).astype(jnp.float32)
        heads_v = all_values.reshape(HIST + CAND, H, HEAD).astype(jnp.float32)
        scores = jnp.einsum('qhd,khd->hqk', heads_q, heads_k) * scale
        spots = jnp.arange(HIST + CAND)
        usable = jnp.where(spots < HIST, spots < hlength, spots - HIST < count)
        scores = jnp.where(usable, scores, negative_fill)
        top = lax.optimization_barrier(jnp.max(scores, axis=-1, keepdims=True))
        expo = jnp.where(usable, jnp.exp(scores - top), 0.0)
        probs = expo / lax.optimization_barrier(jnp.sum(expo, axis=-1, keepdims=True))
        probs_f = lax.optimization_barrier(probs.astype(jnp.bfloat16)).astype(jnp.float32)
        mixed = jnp.einsum('hqk,khd->qhd', probs_f, heads_v).reshape(CAND, D).astype(jnp.bfloat16)
        output = (feats + mixed.astype(jnp.float32)).astype(jnp.bfloat16)
        live = (jnp.arange(CAND) < count).astype(jnp.float32)[:, None]
        grad_out = cot.astype(jnp.float32) * live
        grad_mix = grad_out.astype(jnp.bfloat16)
        heads_g = grad_mix.reshape(CAND, H, HEAD).astype(jnp.float32)
        grad_probs = jnp.einsum('qhd,khd->hqk', heads_g, heads_v)
        row_dot = lax.optimization_barrier(jnp.sum(probs * grad_probs, axis=-1, keepdims=True))
        grad_scores = probs * (grad_probs - row_dot) * scale
        scores_f = lax.optimization_barrier(grad_scores.astype(jnp.bfloat16)).astype(jnp.float32)
        grad_query = jnp.einsum('hqk,khd->qhd', scores_f, heads_k).reshape(CAND, D).astype(jnp.bfloat16)
        grad_key = jnp.einsum('hqk,qhd->khd', scores_f[:, :, HIST:], heads_q).reshape(CAND, D).astype(jnp.bfloat16)
        grad_value = jnp.einsum('hqk,qhd->khd', probs_f[:, :, HIST:], heads_g).reshape(CAND, D).astype(jnp.bfloat16)
        grad_normed = jnp.dot(grad_query, w_query.T, preferred_element_type=jnp.float32)
        grad_normed = grad_normed + jnp.dot(grad_key, w_key.T, preferred_element_type=jnp.float32)
        grad_normed = grad_normed + jnp.dot(grad_value, w_value.T, preferred_element_type=jnp.float32)
        scaled = grad_normed * gains
        grad_feats = grad_out + inv_rms * scaled - feats * inv_rms ** 3 * lax.optimization_barrier(jnp.mean(scaled * feats, axis=-1, keepdims=True))
        grad_gain = lax.optimization_barrier(jnp.sum(grad_normed * feats * inv_rms, axis=0))
        part_q = jnp.dot(normed.T, grad_query, preferred_element_type=jnp.float32)
        part_k = jnp.dot(normed.T, grad_key, preferred_element_type=jnp.float32)
        part_v = jnp.dot(normed.T, grad_value, preferred_element_type=jnp.float32)
        return (output, grad_feats.astype(jnp.bfloat16), part_q, part_k, part_v, grad_gain)
    results = lax.map(per_request, (candidates, counts, hist_keys, hist_values, hist_lengths, cotangent))
    return (results[0], results[1], lax.optimization_barrier(jnp.sum(results[2], 0)), lax.optimization_barrier(jnp.sum(results[3], 0)), lax.optimization_barrier(jnp.sum(results[4], 0)), lax.optimization_barrier(jnp.sum(results[5], 0)))
```

```python
import math

import jax
import jax.numpy as jnp
from jax import lax
from jax.experimental import pallas as pl
from jax.experimental.pallas import tpu as pltpu
from jax.sharding import PartitionSpec as P

D = 1024
H = 16
HEAD = 64
ROWS = 128
PAST = 16
CAND = 2048
KEYS = 2304
BLOCK = ROWS + PAST
BF = jnp.bfloat16
F32 = jnp.float32
DEAD = -1e30
SCALE = 0.125
SCALE2 = SCALE / math.log(2.0)
MIB = 1 << 20


def lanes(shape):
    return lax.broadcasted_iota(jnp.int32, shape, len(shape) - 1)


def rows_of(shape):
    return lax.broadcasted_iota(jnp.int32, shape, len(shape) - 2)


def dot(a, b):
    return jnp.dot(a, b, preferred_element_type=F32)


def swap(x):
    return pltpu.roll(x, 64, 1)


def norm_rows(x, gain):
    inv = lax.rsqrt(jnp.mean(x * x, axis=-1, keepdims=True) + 1e-05)
    return x * inv, inv


def project_kernel(live_ref, x_ref, cot_ref, hk_ref, hv_ref, gain_ref, wq_ref, wk_ref, wv_ref, out_ref, normed_ref):
    @pl.when(pl.program_id(0) == 0)
    def _():
        x = x_ref[...].astype(F32)
        hat, _ = norm_rows(x, None)
        normed_ref[...] = (hat * gain_ref[...]).astype(BF)

    normed = normed_ref[...]
    q = dot(normed, wq_ref[...])
    k = dot(normed, wk_ref[...])
    v = dot(normed, wv_ref[...])
    g = cot_ref[...].astype(F32)
    g = jnp.where(rows_of(g.shape) < live_ref[0], g, 0.0)
    hk = hk_ref[...].astype(F32)
    hv = hv_ref[...].astype(F32)
    low = lanes((ROWS, 128)) < 64
    low_h = lanes((PAST, 128)) < 64
    for p in range(q.shape[1] // 128):
        s = slice(128 * p, 128 * p + 128)
        q1, k1, v1, g1, hk1, hv1 = q[:, s], k[:, s], v[:, s], g[:, s], hk[:, s], hv[:, s]
        a, b = 2 * p, 2 * p + 1
        out_ref[a, :ROWS, :128] = jnp.where(low, q1, swap(k1)).astype(BF)
        out_ref[b, :ROWS, :128] = jnp.where(low, swap(q1), k1).astype(BF)
        out_ref[a, :ROWS, 128:] = jnp.where(low, v1, swap(g1)).astype(BF)
        out_ref[b, :ROWS, 128:] = jnp.where(low, swap(v1), g1).astype(BF)
        out_ref[a, ROWS:, :128] = jnp.where(low_h, 0.0, swap(hk1)).astype(BF)
        out_ref[b, ROWS:, :128] = jnp.where(low_h, 0.0, hk1).astype(BF)
        out_ref[a, ROWS:, 128:] = jnp.where(low_h, hv1, 0.0).astype(BF)
        out_ref[b, ROWS:, 128:] = jnp.where(low_h, swap(hv1), 0.0).astype(BF)


def project(live, x, cot, hk, hv, gain, wq, wk, wv):
    n = 4
    w = D // n
    column = lambda j: (0, j)
    whole = lambda j: (0, 0)
    return pl.pallas_call(
        project_kernel,
        grid=(n,),
        in_specs=[
            pl.BlockSpec(memory_space=pltpu.SMEM),
            pl.BlockSpec((ROWS, D), whole),
            pl.BlockSpec((ROWS, w), column),
            pl.BlockSpec((PAST, w), column),
            pl.BlockSpec((PAST, w), column),
            pl.BlockSpec((1, D), whole),
            pl.BlockSpec((D, w), column),
            pl.BlockSpec((D, w), column),
            pl.BlockSpec((D, w), column),
        ],
        out_specs=pl.BlockSpec((H // n, BLOCK, 256), lambda j: (j, 0, 0)),
        out_shape=jax.ShapeDtypeStruct((H, BLOCK, 256), BF),
        scratch_shapes=[pltpu.VMEM((ROWS, D), BF)],
        compiler_params=pltpu.CompilerParams(vmem_limit_bytes=60 * MIB),
        cost_estimate=pl.CostEstimate(flops=6 * ROWS * D * D, bytes_accessed=8 * MIB, transcendentals=0),
        name="project",
    )(live, x, cot, hk, hv, gain, wq, wk, wv)


QB = 256
KC = 256


def attend_kernel(count_ref, past_ref, in_ref, out_ref, kn_ref, vx_ref, kt_ref, vt_ref, dk_ref, dv_ref, s_ref, p_ref, d_ref):
    count = count_ref[0]
    past = past_ref[0]
    low = lanes((128, 128)) < 64
    top = rows_of((128, 128)) == 0
    ones = jnp.where(rows_of((64, 128)) < 3, 1.0, 0.0).astype(BF)

    for j in range(KEYS // 128):
        if j < H:
            raw = in_ref[j, :ROWS, :]
            dead = lanes((128, 128)) + 128 * j >= count
        else:
            t = j - H
            raw = in_ref[8 * t : 8 * t + 8, ROWS:, :].reshape(128, 256)
            dead = lanes((128, 128)) + 128 * t >= past
        c = slice(128 * j, 128 * j + 128)
        kn_ref[c, :] = raw[:, :128]
        vg = raw[:, 128:].astype(F32)
        vx_ref[c, :] = jnp.where(low, vg, 1.0).astype(BF)
        kt = raw[:, :128].astype(F32).T[64:, :].astype(BF)
        kt_ref[0:64, c] = kt
        kt_ref[64:128, c] = kt
        kt_ref[128:256, c] = jnp.where(top & dead, DEAD, 0.0).astype(BF)
        vt_ref[0:64, c] = vg.T[:64, :].astype(BF)
        vt_ref[64:128, c] = ones
    dk_ref[...] = jnp.zeros_like(dk_ref)
    dv_ref[...] = jnp.zeros_like(dv_ref)

    lane = lanes((QB, 128))
    lowq = lane < 64
    unit = jnp.where(lane == 0, 1.0, 0.0).astype(BF)

    def step(i, carry):
        rows = in_ref[pl.ds(2 * i, 2), :ROWS, :].reshape(QB, 256)
        qk = rows[:, :128].astype(F32)
        vg = rows[:, 128:].astype(F32)
        qs = qk * SCALE2
        hi = qs.astype(BF).astype(F32)
        qx = jnp.concatenate([jnp.where(lowq, hi, swap(qs - hi)).astype(BF), unit], axis=1)
        top = None
        for c in range(KEYS // KC):
            cs = slice(c * KC, c * KC + KC)
            s = dot(qx, kt_ref[:, cs])
            s_ref[:, cs] = s
            for h in range(KC // 128):
                part = s[:, 128 * h : 128 * h + 128]
                top = part if top is None else jnp.maximum(top, part)
        top = jnp.max(top, axis=1, keepdims=True)
        pv = None
        for c in range(KEYS // KC):
            cs = slice(c * KC, c * KC + KC)
            e = jnp.exp2(s_ref[:, cs] - top)
            s_ref[:, cs] = e
            e = e.astype(BF)
            p_ref[:, cs] = e
            t = dot(e, vx_ref[cs, :])
            pv = t if pv is None else pv + t
        inv = 1.0 / jnp.where(lowq, swap(pv), 1.0)
        mixed = pv * inv
        g = (swap(vg) * inv).astype(BF)
        gf = g.astype(F32)
        rd = jnp.sum(jnp.where(lowq, gf * mixed, 0.0), axis=1, keepdims=True)
        r1 = rd.astype(BF).astype(F32)
        r2 = (rd - r1).astype(BF).astype(F32)
        r3 = rd - r1 - r2
        gx = jnp.where(lane == 64, -r1, jnp.where(lane == 65, -r2, jnp.where(lane == 66, -r3, 0.0)))
        gx = jnp.where(lowq, gf, gx).astype(BF)
        gq = None
        for c in range(KEYS // KC):
            cs = slice(c * KC, c * KC + KC)
            ds = (s_ref[:, cs] * dot(gx, vt_ref[:, cs])).astype(BF)
            d_ref[:, cs] = ds
            t = dot(ds, kn_ref[cs, :])
            gq = t if gq is None else gq + t
        both = jnp.where(lowq, mixed, gq * SCALE).T.astype(BF)
        out_ref[2 * i, 0:128, :] = both[:, :128]
        out_ref[2 * i + 1, 0:128, :] = both[:, 128:]
        qt = qk.T[:64, :].astype(BF)
        gt = gf.T[:64, :].astype(BF)
        for c in range(KEYS // KC):
            cs = slice(c * KC, c * KC + KC)
            dk_ref[:, cs] += dot(qt, d_ref[:, cs])
            dv_ref[:, cs] += dot(gt, p_ref[:, cs])
        return carry

    lax.fori_loop(0, CAND // QB, step, 0)
    for j in range(H):
        c = slice(128 * j, 128 * j + 128)
        out_ref[j, 128:192, :] = (dk_ref[:, c] * SCALE).astype(BF)
        out_ref[j, 192:256, :] = dv_ref[:, c].astype(BF)


def attend(count, past, packed):
    smem = pl.BlockSpec(memory_space=pltpu.SMEM)
    vmem = pl.BlockSpec(memory_space=pltpu.VMEM)
    return pl.pallas_call(
        attend_kernel,
        in_specs=[smem, smem, vmem],
        out_specs=vmem,
        out_shape=jax.ShapeDtypeStruct((H, 256, ROWS), BF),
        scratch_shapes=[
            pltpu.VMEM((KEYS, 128), BF),
            pltpu.VMEM((KEYS, 128), BF),
            pltpu.VMEM((256, KEYS), BF),
            pltpu.VMEM((128, KEYS), BF),
            pltpu.VMEM((64, KEYS), F32),
            pltpu.VMEM((64, KEYS), F32),
            pltpu.VMEM((QB, KEYS), F32),
            pltpu.VMEM((QB, KEYS), BF),
            pltpu.VMEM((QB, KEYS), BF),
        ],
        compiler_params=pltpu.CompilerParams(vmem_limit_bytes=60 * MIB),
        cost_estimate=pl.CostEstimate(flops=12 * CAND * KEYS * 256, bytes_accessed=3 * MIB, transcendentals=CAND * KEYS),
        name="attend",
    )(count, past, packed)


def weigh_kernel(x_ref, gain_ref, g_ref, out_ref, acc_ref):
    i = pl.program_id(0)

    @pl.when(i == 0)
    def _():
        acc_ref[...] = jnp.zeros_like(acc_ref)

    hat, _ = norm_rows(x_ref[...].astype(F32), None)
    normed = (hat * gain_ref[...]).astype(BF)
    gt = jnp.concatenate([g_ref[0, 64:, :], g_ref[1, 64:, :]], axis=1)
    acc_ref[0:192, :] += dot(gt, normed)

    @pl.when(i == pl.num_programs(0) - 1)
    def _():
        out_ref[...] = acc_ref[...].T.reshape(128, 8, 256).astype(BF)


def weigh(x, gain, grads):
    return pl.pallas_call(
        weigh_kernel,
        grid=(CAND // 256,),
        in_specs=[
            pl.BlockSpec((256, D), lambda i: (i, 0)),
            pl.BlockSpec((1, D), lambda i: (0, 0)),
            pl.BlockSpec((2, 256, ROWS), lambda i: (i, 0, 0)),
        ],
        out_specs=pl.BlockSpec((128, 8, 256), lambda i: (0, 0, 0)),
        out_shape=jax.ShapeDtypeStruct((128, 8, 256), BF),
        scratch_shapes=[pltpu.VMEM((256, D), F32)],
        compiler_params=pltpu.CompilerParams(vmem_limit_bytes=60 * MIB),
        cost_estimate=pl.CostEstimate(flops=2 * CAND * D * 256, bytes_accessed=6 * MIB, transcendentals=0),
        name="weigh",
    )(x, gain, grads)


def finish_kernel(live_ref, x_ref, cot_ref, gain_ref, g_ref, wq_ref, wk_ref, wv_ref, y_ref, gx_ref, acc_ref):
    t = pl.program_id(0)
    grad = lambda n: g_ref[:, 64 * n : 64 * n + 64, :].reshape(D, ROWS)

    @pl.when(t == 0)
    def _():
        mixed = grad(0).astype(F32).T
        y_ref[...] = (x_ref[...].astype(F32) + mixed).astype(BF)

    c = wq_ref.shape[0]
    total = dot(wq_ref[...], grad(1)) + dot(wk_ref[...], grad(2)) + dot(wv_ref[...], grad(3))
    acc_ref[pl.ds(pl.multiple_of(t * c, c), c), :] = total

    @pl.when(t == pl.num_programs(0) - 1)
    def _():
        x = x_ref[...].astype(F32)
        hat, inv = norm_rows(x, None)
        scaled = acc_ref[...].T * gain_ref[...]
        g = cot_ref[...].astype(F32)
        g = jnp.where(rows_of(g.shape) < live_ref[0], g, 0.0)
        mean = jnp.mean(scaled * x, axis=-1, keepdims=True)
        gx_ref[...] = (g + inv * scaled - x * (inv * inv * inv * mean)).astype(BF)


def finish(live, x, cot, gain, grads, wq, wk, wv):
    n = 4
    w = D // n
    whole = lambda j: (0, 0)
    row = lambda j: (j, 0)
    return pl.pallas_call(
        finish_kernel,
        grid=(n,),
        in_specs=[
            pl.BlockSpec(memory_space=pltpu.SMEM),
            pl.BlockSpec((ROWS, D), whole),
            pl.BlockSpec((ROWS, D), whole),
            pl.BlockSpec((1, D), whole),
            pl.BlockSpec((H, 256, ROWS), lambda j: (0, 0, 0)),
            pl.BlockSpec((w, D), row),
            pl.BlockSpec((w, D), row),
            pl.BlockSpec((w, D), row),
        ],
        out_specs=[pl.BlockSpec((ROWS, D), whole), pl.BlockSpec((ROWS, D), whole)],
        out_shape=[jax.ShapeDtypeStruct((ROWS, D), BF)] * 2,
        scratch_shapes=[pltpu.VMEM((D, ROWS), F32)],
        compiler_params=pltpu.CompilerParams(vmem_limit_bytes=60 * MIB),
        cost_estimate=pl.CostEstimate(flops=6 * ROWS * D * D, bytes_accessed=8 * MIB, transcendentals=0),
        name="finish",
    )(live, x, cot, gain, grads, wq, wk, wv)


def settle_kernel(in_ref, gain_ref, wq_ref, wk_ref, wv_ref, q_ref, k_ref, v_ref, gain_out_ref):
    low = lanes((8, 128)) < 64
    total = None
    for r in range(8):
        part = in_ref[16 * r : 16 * r + 16].astype(F32)
        total = part if total is None else total + part
    for p in range(H // 2):
        s = slice(128 * p, 128 * p + 128)
        a, b = total[2 * p], total[2 * p + 1]
        q_ref[:, s] = jnp.where(low, a[:, :128], swap(b[:, :128]))
        k_ref[:, s] = jnp.where(low, swap(a[:, :128]), b[:, :128])
        v_ref[:, s] = jnp.where(low, a[:, 128:], swap(b[:, 128:]))
    back = q_ref[...] * wq_ref[...].astype(F32) + k_ref[...] * wk_ref[...].astype(F32) + v_ref[...] * wv_ref[...].astype(F32)
    back = jnp.sum(back, axis=1, keepdims=True)
    wide = jnp.broadcast_to(back, (8, 128)).T
    gain_out_ref[...] = wide[0:1, :8] / gain_ref[...]


def settle(parts, gain, wq, wk, wv):
    vmem = pl.BlockSpec(memory_space=pltpu.VMEM)
    return pl.pallas_call(
        settle_kernel,
        in_specs=[vmem] * 5,
        out_specs=[vmem] * 4,
        out_shape=[jax.ShapeDtypeStruct((8, D), F32)] * 3 + [jax.ShapeDtypeStruct((1, 8), F32)],
        compiler_params=pltpu.CompilerParams(vmem_limit_bytes=60 * MIB),
        name="settle",
    )(parts, gain, wq, wk, wv)


def body(candidates, counts, hist_keys, hist_values, hist_lengths, gain, w_query, w_key, w_value, cotangent):
    x, cot = candidates[0], cotangent[0]
    spot = lax.axis_index("list")
    place = lax.axis_index("dp") * 16 + spot
    live = counts - spot * ROWS
    gains = gain[None]
    own = lambda w: lax.dynamic_slice_in_dim(w, place * 8, 8, 0)
    own_gain = lax.dynamic_slice_in_dim(gain, place * 8, 8, 0)[None]
    everyone = lax.all_gather(x, "list", axis=0, tiled=True)
    packed = project(live, x, cot, hist_keys[0], hist_values[0], gains, w_query, w_key, w_value)
    packed = lax.all_to_all(packed, "list", 0, 0, tiled=True)
    grads = attend(counts, hist_lengths, packed)
    back = lax.all_to_all(grads, "list", 0, 0, tiled=True)
    parts = weigh(everyone, gains, grads)
    parts = lax.all_to_all(parts, ("dp", "list"), 0, 0, tiled=True)
    y, grad_x = finish(live, x, cot, gains, back, w_query, w_key, w_value)
    gq, gk, gv, ggain = settle(parts, own_gain, own(w_query), own(w_key), own(w_value))
    return (y[None], grad_x[None], gq, gk, gv, ggain.reshape(8))


def solution(mesh):
    rows = P("dp", "list", None)
    weights = P(("dp", "list"), None)
    return jax.shard_map(
        body,
        mesh=mesh,
        in_specs=(rows, P("dp"), rows, rows, P("dp"), P(), P(), P(), P(), rows),
        out_specs=(rows, rows, weights, weights, weights, P(("dp", "list"))),
        check_vma=False,
    )
```

```python
import math

import jax
import jax.numpy as jnp
from jax import lax
from jax.experimental import pallas as pl
from jax.experimental.pallas import tpu as pltpu
from jax.sharding import PartitionSpec as P

D = 1024
H = 16
HEAD = 64
ROWS = 128
PAST = 16
CAND = 2048
KEYS = 2304
BLOCK = ROWS + PAST
BF = jnp.bfloat16
F32 = jnp.float32
DEAD = -1e30
SCALE = 0.125
SCALE2 = SCALE / math.log(2.0)
MIB = 1 << 20


def lanes(shape):
    return lax.broadcasted_iota(jnp.int32, shape, len(shape) - 1)


def rows_of(shape):
    return lax.broadcasted_iota(jnp.int32, shape, len(shape) - 2)


def dot(a, b):
    return jnp.dot(a, b, preferred_element_type=F32)


def swap(x):
    return pltpu.roll(x, 64, 1)


def inverse_rms(x):
    return lax.rsqrt(jnp.mean(x * x, axis=-1, keepdims=True) + 1e-05)


def norm_rows(x, gain):
    return (x * inverse_rms(x) * gain).astype(BF)


SMEM = pl.BlockSpec(memory_space=pltpu.SMEM)
VMEM = pl.BlockSpec(memory_space=pltpu.VMEM)
ANY = pl.BlockSpec(memory_space=pl.ANY)
WHOLE = pl.BlockSpec()
SOON = pl.CostEstimate(flops=1, bytes_accessed=1, transcendentals=0)


PARTS = 4
WIDE = D // PARTS


def project_kernel(live_ref, place_ref, x_ref, cot_ref, hk_ref, hv_ref, gain_ref, wq_ref, wk_ref, wv_ref, out_ref, own_ref, w_ref, sems):
    copies = [
        [
            pltpu.make_async_copy(w.at[:, pl.ds(j * WIDE, WIDE)], w_ref.at[t, j], sems.at[t, j])
            for t, w in enumerate((wq_ref, wk_ref, wv_ref))
        ]
        for j in range(PARTS)
    ]
    for row in copies:
        for copy in row:
            copy.start()
    normed = norm_rows(x_ref[...].astype(F32), gain_ref[...])
    low = lanes((ROWS, 128)) < 64
    low_h = lanes((PAST, 128)) < 64
    alive = rows_of((ROWS, 128)) < live_ref[0]
    own = pl.ds(pl.multiple_of(place_ref[0] // 2 * 16, 16), 16)
    for j in range(PARTS):
        for copy in copies[j]:
            copy.wait()
        q = dot(normed, w_ref[0, j])
        k = dot(normed, w_ref[1, j])
        v = dot(normed, w_ref[2, j])
        for t in range(3):
            own_ref[16 * t : 16 * t + 16, j * WIDE : j * WIDE + WIDE] = w_ref[t, j, own, :]
        for p in range(WIDE // 128):
            s = slice(128 * p, 128 * p + 128)
            c = slice(j * WIDE + 128 * p, j * WIDE + 128 * p + 128)
            q1, k1, v1 = q[:, s], k[:, s], v[:, s]
            g1 = jnp.where(alive, cot_ref[:, c].astype(F32), 0.0)
            hk1, hv1 = hk_ref[:, c].astype(F32), hv_ref[:, c].astype(F32)
            a = (j * WIDE + 128 * p) // HEAD
            b = a + 1
            out_ref[a, :ROWS, :128] = jnp.where(low, q1, swap(k1)).astype(BF)
            out_ref[b, :ROWS, :128] = jnp.where(low, swap(q1), k1).astype(BF)
            out_ref[a, :ROWS, 128:] = jnp.where(low, v1, swap(g1)).astype(BF)
            out_ref[b, :ROWS, 128:] = jnp.where(low, swap(v1), g1).astype(BF)
            out_ref[a, ROWS:, :128] = jnp.where(low_h, 0.0, swap(hk1)).astype(BF)
            out_ref[b, ROWS:, :128] = jnp.where(low_h, 0.0, hk1).astype(BF)
            out_ref[a, ROWS:, 128:] = jnp.where(low_h, hv1, 0.0).astype(BF)
            out_ref[b, ROWS:, 128:] = jnp.where(low_h, swap(hv1), 0.0).astype(BF)


def project(live, place, x, cot, hk, hv, gain, wq, wk, wv):
    return pl.pallas_call(
        project_kernel,
        in_specs=[SMEM] * 2 + [WHOLE] * 5 + [ANY] * 3,
        out_specs=[WHOLE] * 2,
        out_shape=[jax.ShapeDtypeStruct((H, BLOCK, 256), BF), jax.ShapeDtypeStruct((48, D), BF)],
        scratch_shapes=[pltpu.VMEM((3, PARTS, D, WIDE), BF), pltpu.SemaphoreType.DMA((3, PARTS))],
        compiler_params=pltpu.CompilerParams(vmem_limit_bytes=60 * MIB),
        cost_estimate=pl.CostEstimate(flops=60 * ROWS * D * D, bytes_accessed=8 * MIB, transcendentals=0),
        name="project",
    )(live, place, x, cot, hk, hv, gain, wq, wk, wv)


def gather_kernel(a_ref, b_ref, c_ref, d_ref, gain_ref, out_ref):
    for i, ref in enumerate((a_ref, b_ref, c_ref, d_ref)):
        out_ref[ROWS * i : ROWS * i + ROWS, :] = norm_rows(ref[...].astype(F32), gain_ref[...])


def gather(blocks, gain):
    return pl.pallas_call(
        gather_kernel,
        in_specs=[VMEM] * 5,
        out_specs=VMEM,
        out_shape=jax.ShapeDtypeStruct((4 * ROWS, D), BF),
        cost_estimate=SOON,
        compiler_params=pltpu.CompilerParams(vmem_limit_bytes=16 * MIB),
        name="gather",
    )(*blocks, gain)


QB = 256
KC = 768


def attend_kernel(count_ref, past_ref, in_ref, out_ref, kn_ref, vx_ref, kt_ref, vt_ref, dk_ref, dv_ref, s_ref, p_ref, d_ref):
    count = count_ref[0]
    past = past_ref[0]
    low = lanes((128, 128)) < 64
    top = rows_of((128, 128)) == 0
    ones = jnp.where(rows_of((64, 128)) < 3, 1.0, 0.0).astype(BF)

    for j in range(KEYS // 128):
        if j < H:
            raw = in_ref[j, :ROWS, :]
            dead = lanes((128, 128)) + 128 * j >= count
        else:
            t = j - H
            raw = in_ref[8 * t : 8 * t + 8, ROWS:, :].reshape(128, 256)
            dead = lanes((128, 128)) + 128 * t >= past
        c = slice(128 * j, 128 * j + 128)
        kn_ref[c, :] = raw[:, :128]
        vg = raw[:, 128:].astype(F32)
        vx_ref[c, :] = jnp.where(low, vg, 1.0).astype(BF)
        kt = raw[:, :128].astype(F32).T[64:, :].astype(BF)
        kt_ref[0:64, c] = kt
        kt_ref[64:128, c] = kt
        kt_ref[128:256, c] = jnp.where(top & dead, DEAD, 0.0).astype(BF)
        vt_ref[0:64, c] = vg.T[:64, :].astype(BF)
        vt_ref[64:128, c] = ones
    dk_ref[...] = jnp.zeros_like(dk_ref)
    dv_ref[...] = jnp.zeros_like(dv_ref)

    lane = lanes((QB, 128))
    lowq = lane < 64
    unit = jnp.where(lane == 0, 1.0, 0.0).astype(BF)

    def step(i, carry):
        rows = in_ref[pl.ds(2 * i, 2), :ROWS, :].reshape(QB, 256)
        qk = rows[:, :128].astype(F32)
        vg = rows[:, 128:].astype(F32)
        qs = qk * SCALE2
        hi = qs.astype(BF).astype(F32)
        qx = jnp.concatenate([jnp.where(lowq, hi, swap(qs - hi)).astype(BF), unit], axis=1)
        top = None
        for c in range(KEYS // KC):
            cs = slice(c * KC, c * KC + KC)
            s = dot(qx, kt_ref[:, cs])
            s_ref[:, cs] = s
            for h in range(KC // 128):
                part = s[:, 128 * h : 128 * h + 128]
                top = part if top is None else jnp.maximum(top, part)
        top = jnp.max(top, axis=1, keepdims=True)
        pv = None
        for c in range(KEYS // KC):
            cs = slice(c * KC, c * KC + KC)
            e = jnp.exp2(s_ref[:, cs] - top)
            s_ref[:, cs] = e
            e = e.astype(BF)
            p_ref[:, cs] = e
            t = dot(e, vx_ref[cs, :])
            pv = t if pv is None else pv + t
        inv = 1.0 / jnp.where(lowq, swap(pv), 1.0)
        mixed = pv * inv
        g = (swap(vg) * inv).astype(BF)
        gf = g.astype(F32)
        rd = jnp.sum(jnp.where(lowq, gf * mixed, 0.0), axis=1, keepdims=True)
        r1 = rd.astype(BF).astype(F32)
        r2 = (rd - r1).astype(BF).astype(F32)
        r3 = rd - r1 - r2
        gx = jnp.where(lane == 64, -r1, jnp.where(lane == 65, -r2, jnp.where(lane == 66, -r3, 0.0)))
        gx = jnp.where(lowq, gf, gx).astype(BF)
        gq = None
        for c in range(KEYS // KC):
            cs = slice(c * KC, c * KC + KC)
            ds = (s_ref[:, cs] * dot(gx, vt_ref[:, cs])).astype(BF)
            d_ref[:, cs] = ds
            t = dot(ds, kn_ref[cs, :])
            gq = t if gq is None else gq + t
        both = jnp.where(lowq, mixed, gq * SCALE).T.astype(BF)
        out_ref[2 * i, 0:128, :] = both[:, :128]
        out_ref[2 * i + 1, 0:128, :] = both[:, 128:]
        qt = qk.T[:64, :].astype(BF)
        gt = gf.T[:64, :].astype(BF)
        for c in range(KEYS // KC):
            cs = slice(c * KC, c * KC + KC)
            dk_ref[:, cs] += dot(qt, d_ref[:, cs])
            dv_ref[:, cs] += dot(gt, p_ref[:, cs])
        return carry

    lax.fori_loop(0, CAND // QB, step, 0)
    for j in range(H):
        c = slice(128 * j, 128 * j + 128)
        out_ref[j, 128:192, :] = (dk_ref[:, c] * SCALE).astype(BF)
        out_ref[j, 192:256, :] = dv_ref[:, c].astype(BF)


def attend(count, past, packed):
    return pl.pallas_call(
        attend_kernel,
        in_specs=[SMEM, SMEM, VMEM],
        out_specs=VMEM,
        out_shape=jax.ShapeDtypeStruct((H, 256, ROWS), BF),
        scratch_shapes=[
            pltpu.VMEM((KEYS, 128), BF),
            pltpu.VMEM((KEYS, 128), BF),
            pltpu.VMEM((256, KEYS), BF),
            pltpu.VMEM((128, KEYS), BF),
            pltpu.VMEM((64, KEYS), F32),
            pltpu.VMEM((64, KEYS), F32),
            pltpu.VMEM((QB, KEYS), F32),
            pltpu.VMEM((QB, KEYS), BF),
            pltpu.VMEM((QB, KEYS), BF),
        ],
        compiler_params=pltpu.CompilerParams(vmem_limit_bytes=24 * MIB),
        cost_estimate=pl.CostEstimate(flops=12 * CAND * KEYS * 256, bytes_accessed=3 * MIB, transcendentals=CAND * KEYS),
        name="attend",
    )(count, past, packed)


def weigh_kernel(where_ref, n0, n1, n2, n3, g0, g1, g2, g3, keep_ref, give_ref, acc_ref):
    i = pl.program_id(0)
    left = jnp.concatenate([g[0, 64:, :] for g in (g0, g1, g2, g3)], axis=1)
    right = jnp.concatenate([n[...] for n in (n0, n1, n2, n3)], axis=0)
    part = dot(left, right)

    @pl.when(i == 0)
    def _():
        acc_ref[...] = part

    @pl.when(i > 0)
    def _():
        acc_ref[...] += part

    @pl.when(i == pl.num_programs(0) - 1)
    def _():
        core = where_ref[16]
        for z in range(4):
            mine = pl.ds(pl.multiple_of((2 * z + core) * 128, 128), 128)
            other = pl.ds(pl.multiple_of((2 * z + 1 - core) * 128, 128), 128)
            keep_ref[z] = acc_ref[:, mine]
            give_ref[z] = acc_ref[:, other].astype(BF)


def weigh(where, normed, grads):
    fixed = lambda i, w: (0, 0, 0)
    return pl.pallas_call(
        weigh_kernel,
        grid_spec=pltpu.PrefetchScalarGridSpec(
            num_scalar_prefetch=1,
            grid=(4,),
            in_specs=[pl.BlockSpec((ROWS, D), lambda i, w: (i, 0))] * 4
            + [pl.BlockSpec((1, 256, ROWS), lambda i, w, a=a: (w[4 * a + i], 0, 0)) for a in range(4)],
            out_specs=[pl.BlockSpec((4, 192, 128), fixed), pl.BlockSpec((4, 192, 128), fixed)],
            scratch_shapes=[pltpu.VMEM((192, D), F32)],
        ),
        out_shape=[jax.ShapeDtypeStruct((4, 192, 128), F32), jax.ShapeDtypeStruct((4, 192, 128), BF)],
        compiler_params=pltpu.CompilerParams(vmem_limit_bytes=24 * MIB),
        cost_estimate=SOON,
        name="weigh",
    )(where, *normed, *([grads] * 4))


def pair_kernel(where_ref, keep_ref, came_ref, own_ref, a_ref, b_ref, c_ref):
    z = where_ref[17]
    total = lambda s: keep_ref[(z + s) % 4] + came_ref[(z + s) % 4].astype(F32)
    own_ref[...] = total(0)
    a_ref[...] = total(1).astype(BF)
    b_ref[...] = total(2).astype(BF)
    c_ref[...] = total(3).astype(BF)


def pair(where, keep, came):
    return pl.pallas_call(
        pair_kernel,
        in_specs=[SMEM, VMEM, VMEM],
        out_specs=[VMEM] * 4,
        out_shape=[jax.ShapeDtypeStruct((192, 128), F32)] + [jax.ShapeDtypeStruct((192, 128), BF)] * 3,
        cost_estimate=SOON,
        compiler_params=pltpu.CompilerParams(vmem_limit_bytes=16 * MIB),
        name="pair",
    )(where, keep, came)


def line_kernel(own_ref, a_ref, b_ref, c_ref, out_ref):
    total = own_ref[...] + a_ref[...].astype(F32) + b_ref[...].astype(F32) + c_ref[...].astype(F32)
    total = jnp.concatenate([total, jnp.zeros((64, 128), F32)], axis=0)
    out_ref[...] = total.T.reshape(16, 8, 256)


def line(own, a, b, c):
    return pl.pallas_call(
        line_kernel,
        in_specs=[VMEM] * 4,
        out_specs=VMEM,
        out_shape=jax.ShapeDtypeStruct((16, 8, 256), F32),
        cost_estimate=SOON,
        compiler_params=pltpu.CompilerParams(vmem_limit_bytes=16 * MIB),
        name="line",
    )(own, a, b, c)


def finish_kernel(live_ref, x_ref, cot_ref, gain_ref, g_ref, wq_ref, wk_ref, wv_ref, y_ref, gx_ref, w_ref, acc_ref, sems):
    copies = [
        [
            pltpu.make_async_copy(w.at[pl.ds(j * WIDE, WIDE), :], w_ref.at[t, j], sems.at[t, j])
            for t, w in enumerate((wq_ref, wk_ref, wv_ref))
        ]
        for j in range(PARTS)
    ]
    for row in copies:
        for copy in row:
            copy.start()
    grad = lambda n: g_ref[:, 64 * n : 64 * n + 64, :].reshape(D, ROWS)
    x = x_ref[...].astype(F32)
    y_ref[...] = (x + grad(0).astype(F32).T).astype(BF)
    for j in range(PARTS):
        for copy in copies[j]:
            copy.wait()
        total = dot(w_ref[0, j], grad(1)) + dot(w_ref[1, j], grad(2)) + dot(w_ref[2, j], grad(3))
        acc_ref[:, WIDE * j : WIDE * j + WIDE] = total.T
    inv = inverse_rms(x)
    scaled = acc_ref[...] * gain_ref[...]
    g = cot_ref[...].astype(F32)
    g = jnp.where(rows_of(g.shape) < live_ref[0], g, 0.0)
    mean = jnp.mean(scaled * x, axis=-1, keepdims=True)
    gx_ref[...] = (g + inv * scaled - x * (inv * inv * inv * mean)).astype(BF)


def finish(live, x, cot, gain, grads, wq, wk, wv):
    return pl.pallas_call(
        finish_kernel,
        in_specs=[SMEM] + [WHOLE] * 4 + [ANY] * 3,
        out_specs=[WHOLE] * 2,
        out_shape=[jax.ShapeDtypeStruct((ROWS, D), BF)] * 2,
        scratch_shapes=[
            pltpu.VMEM((3, PARTS, WIDE, D), BF),
            pltpu.VMEM((ROWS, D), F32),
            pltpu.SemaphoreType.DMA((3, PARTS)),
        ],
        compiler_params=pltpu.CompilerParams(vmem_limit_bytes=60 * MIB),
        cost_estimate=pl.CostEstimate(flops=6 * ROWS * D * D, bytes_accessed=8 * MIB, transcendentals=0),
        name="finish",
    )(live, x, cot, gain, grads, wq, wk, wv)


def settle_kernel(place_ref, in_ref, gain_ref, w_ref, q_ref, k_ref, v_ref, gain_out_ref):
    low = lanes((8, 128)) < 64
    for p in range(H // 2):
        s = slice(128 * p, 128 * p + 128)
        a, b = in_ref[2 * p], in_ref[2 * p + 1]
        q_ref[:, s] = jnp.where(low, a[:, :128], swap(b[:, :128]))
        k_ref[:, s] = jnp.where(low, swap(a[:, :128]), b[:, :128])
        v_ref[:, s] = jnp.where(low, a[:, 128:], swap(b[:, 128:]))
    w = w_ref[...].astype(F32)
    odd = jnp.broadcast_to(place_ref[0] % 2, (8, D)) == 1
    back = 0.0
    for t, ref in enumerate((q_ref, k_ref, v_ref)):
        back = back + ref[...] * jnp.where(odd, w[16 * t + 8 : 16 * t + 16], w[16 * t : 16 * t + 8])
    back = jnp.sum(back, axis=1, keepdims=True)
    own = lanes((8, D)) == 8 * place_ref[0] + rows_of((8, D))
    gain = jnp.sum(jnp.where(own, gain_ref[...], 0.0), axis=1, keepdims=True)
    gain_out_ref[...] = jnp.broadcast_to(back / gain, (8, 128)).T[0:1, :8]


def settle(place, parts, gain, weights):
    return pl.pallas_call(
        settle_kernel,
        in_specs=[SMEM, VMEM, VMEM, VMEM],
        out_specs=[WHOLE] * 4,
        out_shape=[jax.ShapeDtypeStruct((8, D), F32)] * 3 + [jax.ShapeDtypeStruct((1, 8), F32)],
        compiler_params=pltpu.CompilerParams(vmem_limit_bytes=16 * MIB),
        name="settle",
    )(place, parts, gain, weights)


def neighbour(first, s):
    pairs = []
    for i in range(128):
        spot = i % 16
        if (i // 16 % 2 == 0) == first:
            spot = spot // 4 * 4 + (spot + s) % 4
        else:
            spot = (spot + 4 * s) % 16
        pairs.append((i, i // 16 * 16 + spot))
    return pairs


def near(a, s):
    return lax.ppermute(a, ("dp", "list"), neighbour(True, s))


def far(a, s):
    return lax.ppermute(a, ("dp", "list"), neighbour(False, s))


def along_z(a, s):
    return lax.ppermute(a, "dp", [(i, (i + 2 * s) % 8) for i in range(8)])


def other_core(a):
    return lax.ppermute(a, "dp", [(i, i ^ 1) for i in range(8)])


def body(candidates, counts, hist_keys, hist_values, hist_lengths, gain, w_query, w_key, w_value, cotangent):
    x, cot = candidates[0], cotangent[0]
    spot, part = lax.axis_index("list"), lax.axis_index("dp")
    live = counts - spot * ROWS
    gains = gain[None]
    a, i = jnp.arange(16) // 4, jnp.arange(16) % 4
    core = part % 2
    dx, dy = jnp.where(core == 0, a, i), jnp.where(core == 0, i, a)
    source = 4 * ((spot // 4 - dx) % 4) + (spot % 4 - dy) % 4
    where = jnp.concatenate([source, jnp.stack([core, part // 2])]).astype(jnp.int32)
    place = (part * 16 + spot).astype(jnp.int32)[None]

    blocks = [x] + [near(x, s) for s in (1, 2, 3)]
    packed, own_weights = project(live, place, x, cot, hist_keys[0], hist_values[0], gains, w_query, w_key, w_value)
    packed, where, *blocks = lax.optimization_barrier((packed, where, *blocks))
    packed = lax.all_to_all(packed, "list", 0, 0, tiled=True)
    normed = gather(blocks, gains)
    normed, packed = lax.optimization_barrier((normed, packed))
    normed = [normed] + [far(normed, s) for s in (1, 2, 3)]
    grads = attend(counts, hist_lengths, packed)
    back = lax.all_to_all(grads, "list", 0, 0, tiled=True)
    keep, give = weigh(where, normed, grads)
    own, *give = pair(where, keep, other_core(give))
    parts = line(own, *[along_z(g, s) for g, s in zip(give, (1, 2, 3))])
    parts, back = lax.optimization_barrier((parts, back))
    parts = lax.all_to_all(parts, "list", 0, 0, tiled=True)
    y, grad_x = finish(live, x, cot, gains, back, w_query, w_key, w_value)
    gq, gk, gv, ggain = settle(place, parts, gains, own_weights)
    return (y[None], grad_x[None], gq, gk, gv, ggain.reshape(8))


def solution(mesh):
    rows = P("dp", "list", None)
    weights = P(("dp", "list"), None)
    return jax.shard_map(
        body,
        mesh=mesh,
        in_specs=(rows, P("dp"), rows, rows, P("dp"), P(), P(), P(), P(), rows),
        out_specs=(rows, rows, weights, weights, weights, P(("dp", "list"))),
        check_vma=False,
    )
```

```python
import math

import jax
import jax.numpy as jnp
from jax import lax
from jax.experimental import pallas as pl
from jax.experimental.pallas import tpu as pltpu
from jax.sharding import PartitionSpec as P

D = 1024
H = 16
HEAD = 64
ROWS = 128
PAST = 16
CAND = 2048
KEYS = 2304
BLOCK = ROWS + PAST
BF = jnp.bfloat16
F32 = jnp.float32
DEAD = -1e30
SCALE = 0.125
SCALE2 = SCALE / math.log(2.0)
MIB = 1 << 20


def lanes(shape):
    return lax.broadcasted_iota(jnp.int32, shape, len(shape) - 1)


def rows_of(shape):
    return lax.broadcasted_iota(jnp.int32, shape, len(shape) - 2)


def dot(a, b):
    return jnp.dot(a, b, preferred_element_type=F32)


def swap(x):
    return pltpu.roll(x, 64, 1)


def inverse_rms(x):
    return lax.rsqrt(jnp.mean(x * x, axis=-1, keepdims=True) + 1e-05)


def norm_rows(x, gain):
    return (x * inverse_rms(x) * gain).astype(BF)


SMEM = pl.BlockSpec(memory_space=pltpu.SMEM)
VMEM = pl.BlockSpec(memory_space=pltpu.VMEM)
ANY = pl.BlockSpec(memory_space=pl.ANY)
WHOLE = pl.BlockSpec()
SOON = pl.CostEstimate(flops=1, bytes_accessed=1, transcendentals=0)


PARTS = 4
WIDE = D // PARTS


def project_kernel(live_ref, place_ref, x_ref, cot_ref, hk_ref, hv_ref, gain_ref, wq_ref, wk_ref, wv_ref, out_ref, own_ref, w_ref, sems):
    copies = [
        [
            pltpu.make_async_copy(w.at[:, pl.ds(j * WIDE, WIDE)], w_ref.at[t, j], sems.at[t, j])
            for t, w in enumerate((wq_ref, wk_ref, wv_ref))
        ]
        for j in range(PARTS)
    ]
    for row in copies:
        for copy in row:
            copy.start()
    normed = norm_rows(x_ref[...].astype(F32), gain_ref[...])
    low = lanes((ROWS, 128)) < 64
    low_h = lanes((PAST, 128)) < 64
    alive = rows_of((ROWS, 128)) < live_ref[0]
    own = pl.ds(pl.multiple_of(place_ref[0] // 2 * 16, 16), 16)
    for j in range(PARTS):
        for copy in copies[j]:
            copy.wait()
        q = dot(normed, w_ref[0, j])
        k = dot(normed, w_ref[1, j])
        v = dot(normed, w_ref[2, j])
        for t in range(3):
            own_ref[16 * t : 16 * t + 16, j * WIDE : j * WIDE + WIDE] = w_ref[t, j, own, :]
        for p in range(WIDE // 128):
            s = slice(128 * p, 128 * p + 128)
            c = slice(j * WIDE + 128 * p, j * WIDE + 128 * p + 128)
            q1, k1, v1 = q[:, s], k[:, s], v[:, s]
            g1 = jnp.where(alive, cot_ref[:, c].astype(F32), 0.0)
            hk1, hv1 = hk_ref[:, c].astype(F32), hv_ref[:, c].astype(F32)
            a = (j * WIDE + 128 * p) // HEAD
            b = a + 1
            out_ref[a, :ROWS, :128] = jnp.where(low, q1, swap(k1)).astype(BF)
            out_ref[b, :ROWS, :128] = jnp.where(low, swap(q1), k1).astype(BF)
            out_ref[a, :ROWS, 128:] = jnp.where(low, v1, swap(g1)).astype(BF)
            out_ref[b, :ROWS, 128:] = jnp.where(low, swap(v1), g1).astype(BF)
            out_ref[a, ROWS:, :128] = jnp.where(low_h, 0.0, swap(hk1)).astype(BF)
            out_ref[b, ROWS:, :128] = jnp.where(low_h, 0.0, hk1).astype(BF)
            out_ref[a, ROWS:, 128:] = jnp.where(low_h, hv1, 0.0).astype(BF)
            out_ref[b, ROWS:, 128:] = jnp.where(low_h, swap(hv1), 0.0).astype(BF)


def project(live, place, x, cot, hk, hv, gain, wq, wk, wv):
    return pl.pallas_call(
        project_kernel,
        in_specs=[SMEM] * 2 + [WHOLE] * 5 + [ANY] * 3,
        out_specs=[WHOLE] * 2,
        out_shape=[jax.ShapeDtypeStruct((H, BLOCK, 256), BF), jax.ShapeDtypeStruct((48, D), BF)],
        scratch_shapes=[pltpu.VMEM((3, PARTS, D, WIDE), BF), pltpu.SemaphoreType.DMA((3, PARTS))],
        compiler_params=pltpu.CompilerParams(vmem_limit_bytes=60 * MIB),
        cost_estimate=pl.CostEstimate(flops=60 * ROWS * D * D, bytes_accessed=8 * MIB, transcendentals=0),
        name="project",
    )(live, place, x, cot, hk, hv, gain, wq, wk, wv)


def gather_kernel(a_ref, b_ref, c_ref, d_ref, gain_ref, out_ref):
    for i, ref in enumerate((a_ref, b_ref, c_ref, d_ref)):
        out_ref[ROWS * i : ROWS * i + ROWS, :] = norm_rows(ref[...].astype(F32), gain_ref[...])


def gather(blocks, gain):
    return pl.pallas_call(
        gather_kernel,
        in_specs=[VMEM] * 5,
        out_specs=VMEM,
        out_shape=jax.ShapeDtypeStruct((4 * ROWS, D), BF),
        cost_estimate=SOON,
        compiler_params=pltpu.CompilerParams(vmem_limit_bytes=16 * MIB),
        name="gather",
    )(*blocks, gain)


QB = 256
KC = 768


def attend_kernel(count_ref, past_ref, in_ref, out_ref, kn_ref, vx_ref, kt_ref, vt_ref, dk_ref, dv_ref, s_ref, p_ref, d_ref):
    count = count_ref[0]
    past = past_ref[0]
    low = lanes((128, 128)) < 64
    top = rows_of((128, 128)) == 0
    ones = jnp.where(rows_of((64, 128)) < 3, 1.0, 0.0).astype(BF)

    for j in range(KEYS // 128):
        if j < H:
            raw = in_ref[j, :ROWS, :]
            dead = lanes((128, 128)) + 128 * j >= count
        else:
            t = j - H
            raw = in_ref[8 * t : 8 * t + 8, ROWS:, :].reshape(128, 256)
            dead = lanes((128, 128)) + 128 * t >= past
        c = slice(128 * j, 128 * j + 128)
        kn_ref[c, :] = raw[:, :128]
        vg = raw[:, 128:].astype(F32)
        vx_ref[c, :] = jnp.where(low, vg, 1.0).astype(BF)
        kt = raw[:, :128].astype(F32).T[64:, :].astype(BF)
        kt_ref[0:64, c] = kt
        kt_ref[64:128, c] = kt
        kt_ref[128:256, c] = jnp.where(top & dead, DEAD, 0.0).astype(BF)
        vt_ref[0:64, c] = vg.T[:64, :].astype(BF)
        vt_ref[64:128, c] = ones
    dk_ref[...] = jnp.zeros_like(dk_ref)
    dv_ref[...] = jnp.zeros_like(dv_ref)

    lane = lanes((QB, 128))
    lowq = lane < 64
    unit = jnp.where(lane == 0, 1.0, 0.0).astype(BF)

    def step(i, carry):
        rows = in_ref[pl.ds(2 * i, 2), :ROWS, :].reshape(QB, 256)
        qk = rows[:, :128].astype(F32)
        vg = rows[:, 128:].astype(F32)
        qs = qk * SCALE2
        hi = qs.astype(BF).astype(F32)
        qx = jnp.concatenate([jnp.where(lowq, hi, swap(qs - hi)).astype(BF), unit], axis=1)
        top = None
        for c in range(KEYS // KC):
            cs = slice(c * KC, c * KC + KC)
            s = dot(qx, kt_ref[:, cs])
            s_ref[:, cs] = s
            for h in range(KC // 128):
                part = s[:, 128 * h : 128 * h + 128]
                top = part if top is None else jnp.maximum(top, part)
        top = jnp.max(top, axis=1, keepdims=True)
        pv = None
        for c in range(KEYS // KC):
            cs = slice(c * KC, c * KC + KC)
            e = jnp.exp2(s_ref[:, cs] - top)
            s_ref[:, cs] = e
            e = e.astype(BF)
            p_ref[:, cs] = e
            t = dot(e, vx_ref[cs, :])
            pv = t if pv is None else pv + t
        inv = 1.0 / jnp.where(lowq, swap(pv), 1.0)
        mixed = pv * inv
        g = (swap(vg) * inv).astype(BF)
        gf = g.astype(F32)
        rd = jnp.sum(jnp.where(lowq, gf * mixed, 0.0), axis=1, keepdims=True)
        r1 = rd.astype(BF).astype(F32)
        r2 = (rd - r1).astype(BF).astype(F32)
        r3 = rd - r1 - r2
        gx = jnp.where(lane == 64, -r1, jnp.where(lane == 65, -r2, jnp.where(lane == 66, -r3, 0.0)))
        gx = jnp.where(lowq, gf, gx).astype(BF)
        gq = None
        for c in range(KEYS // KC):
            cs = slice(c * KC, c * KC + KC)
            ds = (s_ref[:, cs] * dot(gx, vt_ref[:, cs])).astype(BF)
            d_ref[:, cs] = ds
            t = dot(ds, kn_ref[cs, :])
            gq = t if gq is None else gq + t
        both = jnp.where(lowq, mixed, gq * SCALE).T.astype(BF)
        out_ref[2 * i, 0:128, :] = both[:, :128]
        out_ref[2 * i + 1, 0:128, :] = both[:, 128:]
        qt = qk.T[:64, :].astype(BF)
        gt = gf.T[:64, :].astype(BF)
        for c in range(KEYS // KC):
            cs = slice(c * KC, c * KC + KC)
            dk_ref[:, cs] += dot(qt, d_ref[:, cs])
            dv_ref[:, cs] += dot(gt, p_ref[:, cs])
        return carry

    lax.fori_loop(0, CAND // QB, step, 0)
    for j in range(H):
        c = slice(128 * j, 128 * j + 128)
        out_ref[j, 128:192, :] = (dk_ref[:, c] * SCALE).astype(BF)
        out_ref[j, 192:256, :] = dv_ref[:, c].astype(BF)


def attend(count, past, packed):
    return pl.pallas_call(
        attend_kernel,
        in_specs=[SMEM, SMEM, VMEM],
        out_specs=VMEM,
        out_shape=jax.ShapeDtypeStruct((H, 256, ROWS), BF),
        scratch_shapes=[
            pltpu.VMEM((KEYS, 128), BF),
            pltpu.VMEM((KEYS, 128), BF),
            pltpu.VMEM((256, KEYS), BF),
            pltpu.VMEM((128, KEYS), BF),
            pltpu.VMEM((64, KEYS), F32),
            pltpu.VMEM((64, KEYS), F32),
            pltpu.VMEM((QB, KEYS), F32),
            pltpu.VMEM((QB, KEYS), BF),
            pltpu.VMEM((QB, KEYS), BF),
        ],
        compiler_params=pltpu.CompilerParams(vmem_limit_bytes=24 * MIB),
        cost_estimate=pl.CostEstimate(flops=12 * CAND * KEYS * 256, bytes_accessed=3 * MIB, transcendentals=CAND * KEYS),
        name="attend",
    )(count, past, packed)


def weigh_kernel(where_ref, n0, n1, n2, n3, g0, g1, g2, g3, keep_ref, give_ref, acc_ref):
    i = pl.program_id(0)
    left = jnp.concatenate([g[0, 64:, :] for g in (g0, g1, g2, g3)], axis=1)
    right = jnp.concatenate([n[...] for n in (n0, n1, n2, n3)], axis=0)
    part = dot(left, right)

    @pl.when(i == 0)
    def _():
        acc_ref[...] = part

    @pl.when(i > 0)
    def _():
        acc_ref[...] += part

    @pl.when(i == pl.num_programs(0) - 1)
    def _():
        core = where_ref[16]
        for z in range(4):
            mine = pl.ds(pl.multiple_of((2 * z + core) * 128, 128), 128)
            other = pl.ds(pl.multiple_of((2 * z + 1 - core) * 128, 128), 128)
            keep_ref[z] = acc_ref[:, mine]
            give_ref[z] = acc_ref[:, other].astype(BF)


def weigh(where, normed, grads):
    fixed = lambda i, w: (0, 0, 0)
    return pl.pallas_call(
        weigh_kernel,
        grid_spec=pltpu.PrefetchScalarGridSpec(
            num_scalar_prefetch=1,
            grid=(4,),
            in_specs=[pl.BlockSpec((ROWS, D), lambda i, w: (i, 0))] * 4
            + [pl.BlockSpec((1, 256, ROWS), lambda i, w, a=a: (w[4 * a + i], 0, 0)) for a in range(4)],
            out_specs=[pl.BlockSpec((4, 192, 128), fixed), pl.BlockSpec((4, 192, 128), fixed)],
            scratch_shapes=[pltpu.VMEM((192, D), F32)],
        ),
        out_shape=[jax.ShapeDtypeStruct((4, 192, 128), F32), jax.ShapeDtypeStruct((4, 192, 128), BF)],
        compiler_params=pltpu.CompilerParams(vmem_limit_bytes=24 * MIB),
        cost_estimate=SOON,
        name="weigh",
    )(where, *normed, *([grads] * 4))


def pair_kernel(where_ref, keep_ref, came_ref, own_ref, a_ref, b_ref, c_ref):
    z = where_ref[17]
    total = lambda s: keep_ref[(z + s) % 4] + came_ref[(z + s) % 4].astype(F32)
    own_ref[...] = total(0)
    a_ref[...] = total(1).astype(BF)
    b_ref[...] = total(2).astype(BF)
    c_ref[...] = total(3).astype(BF)


def pair(where, keep, came):
    return pl.pallas_call(
        pair_kernel,
        in_specs=[SMEM, VMEM, VMEM],
        out_specs=[VMEM] * 4,
        out_shape=[jax.ShapeDtypeStruct((192, 128), F32)] + [jax.ShapeDtypeStruct((192, 128), BF)] * 3,
        cost_estimate=SOON,
        compiler_params=pltpu.CompilerParams(vmem_limit_bytes=16 * MIB),
        name="pair",
    )(where, keep, came)


def line_kernel(own_ref, a_ref, b_ref, c_ref, out_ref):
    total = own_ref[...] + a_ref[...].astype(F32) + b_ref[...].astype(F32) + c_ref[...].astype(F32)
    total = jnp.concatenate([total, jnp.zeros((64, 128), F32)], axis=0)
    out_ref[...] = total.T.reshape(16, 8, 256)


def line(own, a, b, c):
    return pl.pallas_call(
        line_kernel,
        in_specs=[VMEM] * 4,
        out_specs=VMEM,
        out_shape=jax.ShapeDtypeStruct((16, 8, 256), F32),
        cost_estimate=SOON,
        compiler_params=pltpu.CompilerParams(vmem_limit_bytes=16 * MIB),
        name="line",
    )(own, a, b, c)


def finish_kernel(live_ref, x_ref, cot_ref, gain_ref, g_ref, wq_ref, wk_ref, wv_ref, y_ref, gx_ref, w_ref, acc_ref, sems):
    copies = [
        [
            pltpu.make_async_copy(w.at[pl.ds(j * WIDE, WIDE), :], w_ref.at[t, j], sems.at[t, j])
            for t, w in enumerate((wq_ref, wk_ref, wv_ref))
        ]
        for j in range(PARTS)
    ]
    for row in copies:
        for copy in row:
            copy.start()
    grad = lambda n: g_ref[:, 64 * n : 64 * n + 64, :].reshape(D, ROWS)
    x = x_ref[...].astype(F32)
    y_ref[...] = (x + grad(0).astype(F32).T).astype(BF)
    for j in range(PARTS):
        for copy in copies[j]:
            copy.wait()
        total = dot(w_ref[0, j], grad(1)) + dot(w_ref[1, j], grad(2)) + dot(w_ref[2, j], grad(3))
        acc_ref[:, WIDE * j : WIDE * j + WIDE] = total.T
    inv = inverse_rms(x)
    scaled = acc_ref[...] * gain_ref[...]
    g = cot_ref[...].astype(F32)
    g = jnp.where(rows_of(g.shape) < live_ref[0], g, 0.0)
    mean = jnp.mean(scaled * x, axis=-1, keepdims=True)
    gx_ref[...] = (g + inv * scaled - x * (inv * inv * inv * mean)).astype(BF)


def finish(live, x, cot, gain, grads, wq, wk, wv):
    return pl.pallas_call(
        finish_kernel,
        in_specs=[SMEM] + [WHOLE] * 4 + [ANY] * 3,
        out_specs=[WHOLE] * 2,
        out_shape=[jax.ShapeDtypeStruct((ROWS, D), BF)] * 2,
        scratch_shapes=[
            pltpu.VMEM((3, PARTS, WIDE, D), BF),
            pltpu.VMEM((ROWS, D), F32),
            pltpu.SemaphoreType.DMA((3, PARTS)),
        ],
        compiler_params=pltpu.CompilerParams(vmem_limit_bytes=60 * MIB),
        cost_estimate=pl.CostEstimate(flops=6 * ROWS * D * D, bytes_accessed=8 * MIB, transcendentals=0),
        name="finish",
    )(live, x, cot, gain, grads, wq, wk, wv)


def settle_kernel(place_ref, in_ref, gain_ref, w_ref, q_ref, k_ref, v_ref, gain_out_ref):
    low = lanes((8, 128)) < 64
    for p in range(H // 2):
        s = slice(128 * p, 128 * p + 128)
        a, b = in_ref[2 * p], in_ref[2 * p + 1]
        q_ref[:, s] = jnp.where(low, a[:, :128], swap(b[:, :128]))
        k_ref[:, s] = jnp.where(low, swap(a[:, :128]), b[:, :128])
        v_ref[:, s] = jnp.where(low, a[:, 128:], swap(b[:, 128:]))
    w = w_ref[...].astype(F32)
    odd = jnp.broadcast_to(place_ref[0] % 2, (8, D)) == 1
    back = 0.0
    for t, ref in enumerate((q_ref, k_ref, v_ref)):
        back = back + ref[...] * jnp.where(odd, w[16 * t + 8 : 16 * t + 16], w[16 * t : 16 * t + 8])
    back = jnp.sum(back, axis=1, keepdims=True)
    own = lanes((8, D)) == 8 * place_ref[0] + rows_of((8, D))
    gain = jnp.sum(jnp.where(own, gain_ref[...], 0.0), axis=1, keepdims=True)
    gain_out_ref[...] = jnp.broadcast_to(back / gain, (8, 128)).T[0:1, :8]


def settle(place, parts, gain, weights):
    return pl.pallas_call(
        settle_kernel,
        in_specs=[SMEM, VMEM, VMEM, VMEM],
        out_specs=[WHOLE] * 4,
        out_shape=[jax.ShapeDtypeStruct((8, D), F32)] * 3 + [jax.ShapeDtypeStruct((1, 8), F32)],
        compiler_params=pltpu.CompilerParams(vmem_limit_bytes=16 * MIB),
        name="settle",
    )(place, parts, gain, weights)


def in_plane(a, first, move):
    pairs = []
    for i in range(128):
        spot = i % 16
        if (i // 16 % 2 == 0) == first:
            spot = spot // 4 * 4 + move(spot % 4)
        else:
            spot = move(spot // 4) * 4 + spot % 4
        pairs.append((i, i // 16 * 16 + spot))
    return lax.ppermute(a, ("dp", "list"), pairs)


def along_z(a, s):
    return lax.ppermute(a, "dp", [(i, (i + 2 * s) % 8) for i in range(8)])


def other_core(a):
    return lax.ppermute(a, "dp", [(i, i ^ 1) for i in range(8)])


def body(candidates, counts, hist_keys, hist_values, hist_lengths, gain, w_query, w_key, w_value, cotangent):
    x, cot = candidates[0], cotangent[0]
    spot, part = lax.axis_index("list"), lax.axis_index("dp")
    live = counts - spot * ROWS
    gains = gain[None]
    a, i = jnp.arange(16) // 4, jnp.arange(16) % 4
    core = part % 2
    source = spot ^ jnp.where(core == 0, 4 * a + i, 4 * i + a)
    where = jnp.concatenate([source, jnp.stack([core, part // 2])]).astype(jnp.int32)
    place = (part * 16 + spot).astype(jnp.int32)[None]

    blocks = [x] + [in_plane(x, True, lambda p, s=s: p ^ s) for s in (1, 2, 3)]
    packed, own_weights = project(live, place, x, cot, hist_keys[0], hist_values[0], gains, w_query, w_key, w_value)
    packed, where, *blocks = lax.optimization_barrier((packed, where, *blocks))
    packed = lax.all_to_all(packed, "list", 0, 0, tiled=True)
    normed = gather(blocks, gains)
    normed = [normed] + [in_plane(normed, False, lambda p, s=s: p ^ s) for s in (1, 2, 3)]
    grads = attend(counts, hist_lengths, packed)
    back = lax.all_to_all(grads, "list", 0, 0, tiled=True)
    keep, give = weigh(where, normed, grads)
    own, *give = pair(where, keep, other_core(give))
    parts = line(own, *[along_z(g, s) for g, s in zip(give, (1, 2, 3))])
    parts, back = lax.optimization_barrier((parts, back))
    parts = lax.all_to_all(parts, "list", 0, 0, tiled=True)
    y, grad_x = finish(live, x, cot, gains, back, w_query, w_key, w_value)
    gq, gk, gv, ggain = settle(place, parts, gains, own_weights)
    return (y[None], grad_x[None], gq, gk, gv, ggain.reshape(8))


def solution(mesh):
    rows = P("dp", "list", None)
    weights = P(("dp", "list"), None)
    return jax.shard_map(
        body,
        mesh=mesh,
        in_specs=(rows, P("dp"), rows, rows, P("dp"), P(), P(), P(), P(), rows),
        out_specs=(rows, rows, weights, weights, weights, P(("dp", "list"))),
        check_vma=False,
    )
```

```python
import math

import jax
import jax.numpy as jnp
from jax import lax
from jax.experimental import pallas as pl
from jax.experimental.pallas import tpu as pltpu
from jax.sharding import PartitionSpec as P

D = 1024
H = 16
HEAD = 64
ROWS = 128
PAST = 16
CAND = 2048
KEYS = 2304
BLOCK = ROWS + PAST
BF = jnp.bfloat16
F32 = jnp.float32
DEAD = -1e30
SCALE = 0.125
SCALE2 = SCALE / math.log(2.0)
MIB = 1 << 20


def lanes(shape):
    return lax.broadcasted_iota(jnp.int32, shape, len(shape) - 1)


def rows_of(shape):
    return lax.broadcasted_iota(jnp.int32, shape, len(shape) - 2)


def dot(a, b):
    return jnp.dot(a, b, preferred_element_type=F32)


def swap(x):
    return pltpu.roll(x, 64, 1)


def inverse_rms(x):
    return lax.rsqrt(jnp.mean(x * x, axis=-1, keepdims=True) + 1e-05)


def norm_rows(x, gain):
    return (x * inverse_rms(x) * gain).astype(BF)


SMEM = pl.BlockSpec(memory_space=pltpu.SMEM)
VMEM = pl.BlockSpec(memory_space=pltpu.VMEM)
ANY = pl.BlockSpec(memory_space=pl.ANY)
WHOLE = pl.BlockSpec()
SOON = pl.CostEstimate(flops=1, bytes_accessed=1, transcendentals=0)


PARTS = 4
WIDE = D // PARTS


def project_kernel(live_ref, place_ref, x_ref, cot_ref, hk_ref, hv_ref, gain_ref, wq_ref, wk_ref, wv_ref, out_ref, own_ref, w_ref, sems):
    copies = [
        [
            pltpu.make_async_copy(w.at[:, pl.ds(j * WIDE, WIDE)], w_ref.at[t, j], sems.at[t, j])
            for t, w in enumerate((wq_ref, wk_ref, wv_ref))
        ]
        for j in range(PARTS)
    ]
    for row in copies:
        for copy in row:
            copy.start()
    normed = norm_rows(x_ref[...].astype(F32), gain_ref[...])
    low = lanes((ROWS, 128)) < 64
    low_h = lanes((PAST, 128)) < 64
    alive = rows_of((ROWS, 128)) < live_ref[0]
    own = pl.ds(pl.multiple_of(place_ref[0] // 2 * 16, 16), 16)
    for j in range(PARTS):
        for copy in copies[j]:
            copy.wait()
        q = dot(normed, w_ref[0, j])
        k = dot(normed, w_ref[1, j])
        v = dot(normed, w_ref[2, j])
        for t in range(3):
            own_ref[16 * t : 16 * t + 16, j * WIDE : j * WIDE + WIDE] = w_ref[t, j, own, :]
        for p in range(WIDE // 128):
            s = slice(128 * p, 128 * p + 128)
            c = slice(j * WIDE + 128 * p, j * WIDE + 128 * p + 128)
            q1, k1, v1 = q[:, s], k[:, s], v[:, s]
            g1 = jnp.where(alive, cot_ref[:, c].astype(F32), 0.0)
            hk1, hv1 = hk_ref[:, c].astype(F32), hv_ref[:, c].astype(F32)
            a = (j * WIDE + 128 * p) // HEAD
            b = a + 1
            out_ref[a, :ROWS, :128] = jnp.where(low, q1, swap(k1)).astype(BF)
            out_ref[b, :ROWS, :128] = jnp.where(low, swap(q1), k1).astype(BF)
            out_ref[a, :ROWS, 128:] = jnp.where(low, v1, swap(g1)).astype(BF)
            out_ref[b, :ROWS, 128:] = jnp.where(low, swap(v1), g1).astype(BF)
            out_ref[a, ROWS:, :128] = jnp.where(low_h, 0.0, swap(hk1)).astype(BF)
            out_ref[b, ROWS:, :128] = jnp.where(low_h, 0.0, hk1).astype(BF)
            out_ref[a, ROWS:, 128:] = jnp.where(low_h, hv1, 0.0).astype(BF)
            out_ref[b, ROWS:, 128:] = jnp.where(low_h, swap(hv1), 0.0).astype(BF)


def project(live, place, x, cot, hk, hv, gain, wq, wk, wv):
    return pl.pallas_call(
        project_kernel,
        in_specs=[SMEM] * 2 + [WHOLE] * 5 + [ANY] * 3,
        out_specs=[WHOLE] * 2,
        out_shape=[jax.ShapeDtypeStruct((H, BLOCK, 256), BF), jax.ShapeDtypeStruct((48, D), BF)],
        scratch_shapes=[pltpu.VMEM((3, PARTS, D, WIDE), BF), pltpu.SemaphoreType.DMA((3, PARTS))],
        compiler_params=pltpu.CompilerParams(vmem_limit_bytes=60 * MIB),
        cost_estimate=pl.CostEstimate(flops=60 * ROWS * D * D, bytes_accessed=8 * MIB, transcendentals=0),
        name="project",
    )(live, place, x, cot, hk, hv, gain, wq, wk, wv)


def gather_kernel(a_ref, b_ref, c_ref, d_ref, gain_ref, out_ref):
    for i, ref in enumerate((a_ref, b_ref, c_ref, d_ref)):
        out_ref[ROWS * i : ROWS * i + ROWS, :] = norm_rows(ref[...].astype(F32), gain_ref[...])


def gather(blocks, gain):
    return pl.pallas_call(
        gather_kernel,
        in_specs=[VMEM] * 5,
        out_specs=VMEM,
        out_shape=jax.ShapeDtypeStruct((4 * ROWS, D), BF),
        cost_estimate=SOON,
        compiler_params=pltpu.CompilerParams(vmem_limit_bytes=16 * MIB),
        name="gather",
    )(*blocks, gain)


QB = 256
KC = 2304


def attend_kernel(count_ref, past_ref, in_ref, out_ref, kn_ref, vx_ref, kt_ref, vt_ref, dk_ref, dv_ref, s_ref, p_ref, d_ref):
    count = count_ref[0]
    past = past_ref[0]
    low = lanes((128, 128)) < 64
    top = rows_of((64, 128)) == 0
    ones = jnp.where(rows_of((64, 128)) < 3, 1.0, 0.0).astype(BF)

    for j in range(KEYS // 128):
        if j < H:
            raw = in_ref[j, :ROWS, :]
            dead = lanes((64, 128)) + 128 * j >= count
        else:
            t = j - H
            raw = in_ref[8 * t : 8 * t + 8, ROWS:, :].reshape(128, 256)
            dead = lanes((64, 128)) + 128 * t >= past
        c = slice(128 * j, 128 * j + 128)
        kn_ref[c, :] = raw[:, :128]
        qk = raw[:, :128].astype(F32)
        vg = raw[:, 128:].astype(F32)
        vx_ref[c, :] = jnp.where(low, vg, 1.0).astype(BF)
        turned = jnp.where(low, vg, qk).T.astype(BF)
        vt_ref[0:64, c] = turned[:64, :]
        vt_ref[64:128, c] = ones
        kt_ref[0:64, c] = turned[64:, :]
        kt_ref[64:128, c] = jnp.where(top & dead, DEAD, 0.0).astype(BF)

    lane = lanes((QB, 128))
    lowq = lane < 64
    unit = jnp.where(lane == 64, 1.0, 0.0)

    blocks = CAND // QB
    chunks = [slice(c, c + KC) for c in range(0, KEYS, KC)]

    def load(i):
        rows = in_ref[2 * i : 2 * i + 2, :ROWS, :].reshape(QB, 256)
        return rows[:, :128].astype(F32), rows[:, 128:].astype(F32)

    def scores(i, qx, cs, top):
        s = dot(qx, kt_ref[:, cs])
        s_ref[i % 2, :, cs] = s
        for h in range(KC // 128):
            part = s[:, 128 * h : 128 * h + 128]
            top = part if top is None else jnp.maximum(top, part)
        return top

    def left(qk):
        return jnp.where(lowq, qk, unit).astype(BF)

    def collect(i, turned, cs):
        dk, dv = dot(turned[64:, :], d_ref[i % 2, :, cs]), dot(turned[:64, :], p_ref[i % 2, :, cs])
        dk_ref[:, cs] = dk if i == 0 else dk_ref[:, cs] + dk
        dv_ref[:, cs] = dv if i == 0 else dv_ref[:, cs] + dv

    qk, vg = load(0)
    qx, top = left(qk), None
    for cs in chunks:
        top = scores(0, qx, cs, top)
    turned = None
    for i in range(blocks):
        top = jnp.max(top, axis=1, keepdims=True)
        pv = None
        for cs in chunks:
            e = jnp.exp2((s_ref[i % 2, :, cs] - top) * SCALE2)
            s_ref[i % 2, :, cs] = e
            e = e.astype(BF)
            p_ref[i % 2, :, cs] = e
            part = dot(e, vx_ref[cs, :])
            pv = part if pv is None else pv + part
            if i > 0:
                collect(i - 1, turned, cs)
        inv = 1.0 / jnp.where(lowq, swap(pv), 1.0)
        mixed = pv * inv
        g = (swap(vg) * inv).astype(BF)
        gf = g.astype(F32)
        rd = jnp.sum(jnp.where(lowq, gf * mixed, 0.0), axis=1, keepdims=True)
        r1 = rd.astype(BF).astype(F32)
        r2 = (rd - r1).astype(BF).astype(F32)
        r3 = rd - r1 - r2
        gx = jnp.where(lane == 64, -r1, jnp.where(lane == 65, -r2, jnp.where(lane == 66, -r3, 0.0)))
        gx = jnp.where(lowq, gf, gx).astype(BF)
        turned = jnp.where(lowq, gf, swap(qk)).T.astype(BF)
        more = i + 1 < blocks
        if more:
            qk, vg = load(i + 1)
            qx = left(qk)
        gq, top = None, None
        for cs in chunks:
            dp = dot(gx, vt_ref[:, cs])
            if more:
                top = scores(i + 1, qx, cs, top)
            ds = (s_ref[i % 2, :, cs] * dp).astype(BF)
            d_ref[i % 2, :, cs] = ds
            part = dot(ds, kn_ref[cs, :])
            gq = part if gq is None else gq + part
        both = jnp.where(lowq, mixed, gq * SCALE).T.astype(BF)
        out_ref[2 * i, 0:128, :] = both[:, :128]
        out_ref[2 * i + 1, 0:128, :] = both[:, 128:]
    for cs in chunks:
        collect(blocks - 1, turned, cs)
    for j in range(H):
        c = slice(128 * j, 128 * j + 128)
        out_ref[j, 128:192, :] = (dk_ref[:, c] * SCALE).astype(BF)
        out_ref[j, 192:256, :] = dv_ref[:, c].astype(BF)


def attend(count, past, packed):
    return pl.pallas_call(
        attend_kernel,
        in_specs=[SMEM, SMEM, VMEM],
        out_specs=VMEM,
        out_shape=jax.ShapeDtypeStruct((H, 256, ROWS), BF),
        scratch_shapes=[
            pltpu.VMEM((KEYS, 128), BF),
            pltpu.VMEM((KEYS, 128), BF),
            pltpu.VMEM((128, KEYS), BF),
            pltpu.VMEM((128, KEYS), BF),
            pltpu.VMEM((64, KEYS), F32),
            pltpu.VMEM((64, KEYS), F32),
            pltpu.VMEM((2, QB, KEYS), F32),
            pltpu.VMEM((2, QB, KEYS), BF),
            pltpu.VMEM((2, QB, KEYS), BF),
        ],
        compiler_params=pltpu.CompilerParams(vmem_limit_bytes=24 * MIB),
        cost_estimate=pl.CostEstimate(flops=12 * CAND * KEYS * 256, bytes_accessed=3 * MIB, transcendentals=CAND * KEYS),
        name="attend",
    )(count, past, packed)


def weigh_kernel(where_ref, n0, n1, n2, n3, g0, g1, g2, g3, keep_ref, give_ref, acc_ref):
    i = pl.program_id(0)
    left = jnp.concatenate([g[0, 64:, :] for g in (g0, g1, g2, g3)], axis=1)
    right = jnp.concatenate([n[...] for n in (n0, n1, n2, n3)], axis=0)
    part = dot(left, right)

    @pl.when(i == 0)
    def _():
        acc_ref[...] = part

    @pl.when(i > 0)
    def _():
        acc_ref[...] += part

    @pl.when(i == pl.num_programs(0) - 1)
    def _():
        core = where_ref[16]
        for z in range(4):
            mine = pl.ds(pl.multiple_of((2 * z + core) * 128, 128), 128)
            other = pl.ds(pl.multiple_of((2 * z + 1 - core) * 128, 128), 128)
            keep_ref[z] = acc_ref[:, mine]
            give_ref[z] = acc_ref[:, other].astype(BF)


def weigh(where, normed, grads):
    fixed = lambda i, w: (0, 0, 0)
    return pl.pallas_call(
        weigh_kernel,
        grid_spec=pltpu.PrefetchScalarGridSpec(
            num_scalar_prefetch=1,
            grid=(4,),
            in_specs=[pl.BlockSpec((ROWS, D), lambda i, w: (i, 0))] * 4
            + [pl.BlockSpec((1, 256, ROWS), lambda i, w, a=a: (w[4 * a + i], 0, 0)) for a in range(4)],
            out_specs=[pl.BlockSpec((4, 192, 128), fixed), pl.BlockSpec((4, 192, 128), fixed)],
            scratch_shapes=[pltpu.VMEM((192, D), F32)],
        ),
        out_shape=[jax.ShapeDtypeStruct((4, 192, 128), F32), jax.ShapeDtypeStruct((4, 192, 128), BF)],
        compiler_params=pltpu.CompilerParams(vmem_limit_bytes=24 * MIB),
        cost_estimate=SOON,
        name="weigh",
    )(where, *normed, *([grads] * 4))


def pair_kernel(where_ref, keep_ref, came_ref, own_ref, a_ref, b_ref, c_ref):
    z = where_ref[17]
    total = lambda s: keep_ref[(z + s) % 4] + came_ref[(z + s) % 4].astype(F32)
    own_ref[...] = total(0)
    a_ref[...] = total(1).astype(BF)
    b_ref[...] = total(2).astype(BF)
    c_ref[...] = total(3).astype(BF)


def pair(where, keep, came):
    return pl.pallas_call(
        pair_kernel,
        in_specs=[SMEM, VMEM, VMEM],
        out_specs=[VMEM] * 4,
        out_shape=[jax.ShapeDtypeStruct((192, 128), F32)] + [jax.ShapeDtypeStruct((192, 128), BF)] * 3,
        cost_estimate=SOON,
        compiler_params=pltpu.CompilerParams(vmem_limit_bytes=16 * MIB),
        name="pair",
    )(where, keep, came)


def line_kernel(own_ref, a_ref, b_ref, c_ref, out_ref):
    total = own_ref[...] + a_ref[...].astype(F32) + b_ref[...].astype(F32) + c_ref[...].astype(F32)
    total = jnp.concatenate([total, jnp.zeros((64, 128), F32)], axis=0)
    out_ref[...] = total.T.reshape(16, 8, 256)


def line(own, a, b, c):
    return pl.pallas_call(
        line_kernel,
        in_specs=[VMEM] * 4,
        out_specs=VMEM,
        out_shape=jax.ShapeDtypeStruct((16, 8, 256), F32),
        cost_estimate=SOON,
        compiler_params=pltpu.CompilerParams(vmem_limit_bytes=16 * MIB),
        name="line",
    )(own, a, b, c)


def finish_kernel(live_ref, x_ref, cot_ref, gain_ref, g_ref, wq_ref, wk_ref, wv_ref, y_ref, gx_ref, w_ref, acc_ref, sems):
    copies = [
        [
            pltpu.make_async_copy(w.at[pl.ds(j * WIDE, WIDE), :], w_ref.at[t, j], sems.at[t, j])
            for t, w in enumerate((wq_ref, wk_ref, wv_ref))
        ]
        for j in range(PARTS)
    ]
    for row in copies:
        for copy in row:
            copy.start()
    grad = lambda n: g_ref[:, 64 * n : 64 * n + 64, :].reshape(D, ROWS)
    x = x_ref[...].astype(F32)
    y_ref[...] = (x + grad(0).astype(F32).T).astype(BF)
    for j in range(PARTS):
        for copy in copies[j]:
            copy.wait()
        total = dot(w_ref[0, j], grad(1)) + dot(w_ref[1, j], grad(2)) + dot(w_ref[2, j], grad(3))
        acc_ref[:, WIDE * j : WIDE * j + WIDE] = total.T
    inv = inverse_rms(x)
    scaled = acc_ref[...] * gain_ref[...]
    g = cot_ref[...].astype(F32)
    g = jnp.where(rows_of(g.shape) < live_ref[0], g, 0.0)
    mean = jnp.mean(scaled * x, axis=-1, keepdims=True)
    gx_ref[...] = (g + inv * scaled - x * (inv * inv * inv * mean)).astype(BF)


def finish(live, x, cot, gain, grads, wq, wk, wv):
    return pl.pallas_call(
        finish_kernel,
        in_specs=[SMEM] + [WHOLE] * 4 + [ANY] * 3,
        out_specs=[WHOLE] * 2,
        out_shape=[jax.ShapeDtypeStruct((ROWS, D), BF)] * 2,
        scratch_shapes=[
            pltpu.VMEM((3, PARTS, WIDE, D), BF),
            pltpu.VMEM((ROWS, D), F32),
            pltpu.SemaphoreType.DMA((3, PARTS)),
        ],
        compiler_params=pltpu.CompilerParams(vmem_limit_bytes=60 * MIB),
        cost_estimate=pl.CostEstimate(flops=6 * ROWS * D * D, bytes_accessed=8 * MIB, transcendentals=0),
        name="finish",
    )(live, x, cot, gain, grads, wq, wk, wv)


def settle_kernel(place_ref, in_ref, gain_ref, w_ref, q_ref, k_ref, v_ref, gain_out_ref):
    low = lanes((8, 128)) < 64
    for p in range(H // 2):
        s = slice(128 * p, 128 * p + 128)
        a, b = in_ref[2 * p], in_ref[2 * p + 1]
        q_ref[:, s] = jnp.where(low, a[:, :128], swap(b[:, :128]))
        k_ref[:, s] = jnp.where(low, swap(a[:, :128]), b[:, :128])
        v_ref[:, s] = jnp.where(low, a[:, 128:], swap(b[:, 128:]))
    w = w_ref[...].astype(F32)
    odd = jnp.broadcast_to(place_ref[0] % 2, (8, D)) == 1
    back = 0.0
    for t, ref in enumerate((q_ref, k_ref, v_ref)):
        back = back + ref[...] * jnp.where(odd, w[16 * t + 8 : 16 * t + 16], w[16 * t : 16 * t + 8])
    back = jnp.sum(back, axis=1, keepdims=True)
    own = lanes((8, D)) == 8 * place_ref[0] + rows_of((8, D))
    gain = jnp.sum(jnp.where(own, gain_ref[...], 0.0), axis=1, keepdims=True)
    gain_out_ref[...] = jnp.broadcast_to(back / gain, (8, 128)).T[0:1, :8]


def settle(place, parts, gain, weights):
    return pl.pallas_call(
        settle_kernel,
        in_specs=[SMEM, VMEM, VMEM, VMEM],
        out_specs=[WHOLE] * 4,
        out_shape=[jax.ShapeDtypeStruct((8, D), F32)] * 3 + [jax.ShapeDtypeStruct((1, 8), F32)],
        compiler_params=pltpu.CompilerParams(vmem_limit_bytes=16 * MIB),
        name="settle",
    )(place, parts, gain, weights)


def in_plane(a, first, move):
    pairs = []
    for i in range(128):
        spot = i % 16
        if (i // 16 % 2 == 0) == first:
            spot = spot // 4 * 4 + move(spot % 4)
        else:
            spot = move(spot // 4) * 4 + spot % 4
        pairs.append((i, i // 16 * 16 + spot))
    return lax.ppermute(a, ("dp", "list"), pairs)


def along_z(a, s):
    return lax.ppermute(a, "dp", [(i, (i + 2 * s) % 8) for i in range(8)])


def other_core(a):
    return lax.ppermute(a, "dp", [(i, i ^ 1) for i in range(8)])


def body(candidates, counts, hist_keys, hist_values, hist_lengths, gain, w_query, w_key, w_value, cotangent):
    x, cot = candidates[0], cotangent[0]
    spot, part = lax.axis_index("list"), lax.axis_index("dp")
    live = counts - spot * ROWS
    gains = gain[None]
    a, i = jnp.arange(16) // 4, jnp.arange(16) % 4
    core = part % 2
    source = spot ^ jnp.where(core == 0, 4 * a + i, 4 * i + a)
    where = jnp.concatenate([source, jnp.stack([core, part // 2])]).astype(jnp.int32)
    place = (part * 16 + spot).astype(jnp.int32)[None]

    blocks = [x] + [in_plane(x, True, lambda p, s=s: p ^ s) for s in (1, 2, 3)]
    packed, own_weights = project(live, place, x, cot, hist_keys[0], hist_values[0], gains, w_query, w_key, w_value)
    packed, where, *blocks = lax.optimization_barrier((packed, where, *blocks))
    packed = lax.all_to_all(packed, "list", 0, 0, tiled=True)
    normed = gather(blocks, gains)
    normed = [normed] + [in_plane(normed, False, lambda p, s=s: p ^ s) for s in (1, 2, 3)]
    grads = attend(counts, hist_lengths, packed)
    back = lax.all_to_all(grads, "list", 0, 0, tiled=True)
    keep, give = weigh(where, normed, grads)
    own, *give = pair(where, keep, other_core(give))
    parts = line(own, *[along_z(g, s) for g, s in zip(give, (1, 2, 3))])
    parts, back = lax.optimization_barrier((parts, back))
    parts = lax.all_to_all(parts, "list", 0, 0, tiled=True)
    y, grad_x = finish(live, x, cot, gains, back, w_query, w_key, w_value)
    gq, gk, gv, ggain = settle(place, parts, gains, own_weights)
    return (y[None], grad_x[None], gq, gk, gv, ggain.reshape(8))


def solution(mesh):
    rows = P("dp", "list", None)
    weights = P(("dp", "list"), None)
    return jax.shard_map(
        body,
        mesh=mesh,
        in_specs=(rows, P("dp"), rows, rows, P("dp"), P(), P(), P(), P(), rows),
        out_specs=(rows, rows, weights, weights, weights, P(("dp", "list"))),
        check_vma=False,
    )
```

```python
import math

import jax
import jax.numpy as jnp
from jax import lax
from jax.experimental import pallas as pl
from jax.experimental.pallas import tpu as pltpu
from jax.sharding import PartitionSpec as P

D = 1024
H = 16
HEAD = 64
ROWS = 128
PAST = 16
CAND = 2048
KEYS = 2304
BLOCK = ROWS + PAST
BF = jnp.bfloat16
F32 = jnp.float32
DEAD = -1e30
SCALE = 0.125
SCALE2 = SCALE / math.log(2.0)
MIB = 1 << 20


def lanes(shape):
    return lax.broadcasted_iota(jnp.int32, shape, len(shape) - 1)


def rows_of(shape):
    return lax.broadcasted_iota(jnp.int32, shape, len(shape) - 2)


def dot(a, b):
    return jnp.dot(a, b, preferred_element_type=F32)


def swap(x):
    return pltpu.roll(x, 64, 1)


def inverse_rms(x):
    return lax.rsqrt(jnp.mean(x * x, axis=-1, keepdims=True) + 1e-05)


def norm_rows(x, gain):
    return (x * inverse_rms(x) * gain).astype(BF)


SMEM = pl.BlockSpec(memory_space=pltpu.SMEM)
VMEM = pl.BlockSpec(memory_space=pltpu.VMEM)
ANY = pl.BlockSpec(memory_space=pl.ANY)
WHOLE = pl.BlockSpec()
SOON = pl.CostEstimate(flops=1, bytes_accessed=1, transcendentals=0)


PARTS = 4
WIDE = D // PARTS


def project_kernel(live_ref, place_ref, x_ref, cot_ref, hk_ref, hv_ref, gain_ref, wq_ref, wk_ref, wv_ref, out_ref, own_ref, w_ref, sems):
    copies = [
        [
            pltpu.make_async_copy(w.at[:, pl.ds(j * WIDE, WIDE)], w_ref.at[t, j], sems.at[t, j])
            for t, w in enumerate((wq_ref, wk_ref, wv_ref))
        ]
        for j in range(PARTS)
    ]
    for row in copies:
        for copy in row:
            copy.start()
    normed = norm_rows(x_ref[...].astype(F32), gain_ref[...])
    low = lanes((ROWS, 128)) < 64
    low_h = lanes((PAST, 128)) < 64
    alive = rows_of((ROWS, 128)) < live_ref[0]
    own = pl.ds(pl.multiple_of(place_ref[0] // 2 * 16, 16), 16)
    for j in range(PARTS):
        for copy in copies[j]:
            copy.wait()
        q = dot(normed, w_ref[0, j])
        k = dot(normed, w_ref[1, j])
        v = dot(normed, w_ref[2, j])
        for t in range(3):
            own_ref[16 * t : 16 * t + 16, j * WIDE : j * WIDE + WIDE] = w_ref[t, j, own, :]
        for p in range(WIDE // 128):
            s = slice(128 * p, 128 * p + 128)
            c = slice(j * WIDE + 128 * p, j * WIDE + 128 * p + 128)
            q1, k1, v1 = q[:, s], k[:, s], v[:, s]
            g1 = jnp.where(alive, cot_ref[:, c].astype(F32), 0.0)
            hk1, hv1 = hk_ref[:, c].astype(F32), hv_ref[:, c].astype(F32)
            a = (j * WIDE + 128 * p) // HEAD
            b = a + 1
            out_ref[a, :ROWS, :128] = jnp.where(low, q1, swap(k1)).astype(BF)
            out_ref[b, :ROWS, :128] = jnp.where(low, swap(q1), k1).astype(BF)
            out_ref[a, :ROWS, 128:] = jnp.where(low, v1, swap(g1)).astype(BF)
            out_ref[b, :ROWS, 128:] = jnp.where(low, swap(v1), g1).astype(BF)
            out_ref[a, ROWS:, :128] = jnp.where(low_h, 0.0, swap(hk1)).astype(BF)
            out_ref[b, ROWS:, :128] = jnp.where(low_h, 0.0, hk1).astype(BF)
            out_ref[a, ROWS:, 128:] = jnp.where(low_h, hv1, 0.0).astype(BF)
            out_ref[b, ROWS:, 128:] = jnp.where(low_h, swap(hv1), 0.0).astype(BF)


def project(live, place, x, cot, hk, hv, gain, wq, wk, wv):
    return pl.pallas_call(
        project_kernel,
        in_specs=[SMEM] * 2 + [WHOLE] * 5 + [ANY] * 3,
        out_specs=[WHOLE] * 2,
        out_shape=[jax.ShapeDtypeStruct((H, BLOCK, 256), BF), jax.ShapeDtypeStruct((48, D), BF)],
        scratch_shapes=[pltpu.VMEM((3, PARTS, D, WIDE), BF), pltpu.SemaphoreType.DMA((3, PARTS))],
        compiler_params=pltpu.CompilerParams(vmem_limit_bytes=60 * MIB),
        cost_estimate=pl.CostEstimate(flops=60 * ROWS * D * D, bytes_accessed=8 * MIB, transcendentals=0),
        name="project",
    )(live, place, x, cot, hk, hv, gain, wq, wk, wv)


def gather_kernel(a_ref, b_ref, c_ref, d_ref, gain_ref, out_ref):
    for i, ref in enumerate((a_ref, b_ref, c_ref, d_ref)):
        out_ref[ROWS * i : ROWS * i + ROWS, :] = norm_rows(ref[...].astype(F32), gain_ref[...])


def gather(blocks, gain):
    return pl.pallas_call(
        gather_kernel,
        in_specs=[VMEM] * 5,
        out_specs=VMEM,
        out_shape=jax.ShapeDtypeStruct((4 * ROWS, D), BF),
        cost_estimate=SOON,
        compiler_params=pltpu.CompilerParams(vmem_limit_bytes=16 * MIB),
        name="gather",
    )(*blocks, gain)


QB = 256
KC = 2304


def attend_kernel(count_ref, past_ref, in_ref, out_ref, kn_ref, vx_ref, kt_ref, vt_ref, dk_ref, dv_ref, s_ref, p_ref, d_ref):
    count = count_ref[0]
    past = past_ref[0]
    low = lanes((128, 128)) < 64
    top = rows_of((64, 128)) == 0
    ones = jnp.where(rows_of((64, 128)) < 3, 1.0, 0.0).astype(BF)

    for j in range(KEYS // 128):
        if j < H:
            raw = in_ref[j, :ROWS, :]
            dead = lanes((64, 128)) + 128 * j >= count
        else:
            t = j - H
            raw = in_ref[8 * t : 8 * t + 8, ROWS:, :].reshape(128, 256)
            dead = lanes((64, 128)) + 128 * t >= past
        c = slice(128 * j, 128 * j + 128)
        kn_ref[c, :] = raw[:, :128]
        qk = raw[:, :128].astype(F32)
        vg = raw[:, 128:].astype(F32)
        vx_ref[c, :] = jnp.where(low, vg, 1.0).astype(BF)
        turned = jnp.where(low, vg, qk).T.astype(BF)
        vt_ref[0:64, c] = turned[:64, :]
        vt_ref[64:128, c] = ones
        kt_ref[0:64, c] = turned[64:, :]
        kt_ref[64:128, c] = jnp.where(top & dead, DEAD, 0.0).astype(BF)

    lane = lanes((QB, 128))
    lowq = lane < 64
    unit = jnp.where(lane == 64, 1.0, 0.0)

    blocks = CAND // QB
    chunks = [slice(c, c + KC) for c in range(0, KEYS, KC)]

    def load(i):
        rows = in_ref[2 * i : 2 * i + 2, :ROWS, :].reshape(QB, 256)
        return rows[:, :128].astype(F32), rows[:, 128:].astype(F32)

    def scores(i, qx, cs, top):
        s = dot(qx, kt_ref[:, cs])
        s_ref[i % 2, :, cs] = s
        for h in range(KC // 128):
            part = s[:, 128 * h : 128 * h + 128]
            top = part if top is None else jnp.maximum(top, part)
        return top

    def left(qk):
        return jnp.where(lowq, qk, unit).astype(BF)

    def collect(i, turned, cs):
        dk, dv = dot(turned[64:, :], d_ref[i % 2, :, cs]), dot(turned[:64, :], p_ref[i % 2, :, cs])
        dk_ref[:, cs] = dk if i == 0 else dk_ref[:, cs] + dk
        dv_ref[:, cs] = dv if i == 0 else dv_ref[:, cs] + dv

    qk, vg = load(0)
    qx, top = left(qk), None
    for cs in chunks:
        top = scores(0, qx, cs, top)
    turned = None
    for i in range(blocks):
        top = jnp.max(top, axis=1, keepdims=True)
        pv = None
        for cs in chunks:
            e = jnp.exp2((s_ref[i % 2, :, cs] - top) * SCALE2)
            s_ref[i % 2, :, cs] = e
            e = e.astype(BF)
            p_ref[i % 2, :, cs] = e
            part = dot(e, vx_ref[cs, :])
            pv = part if pv is None else pv + part
            if i > 0:
                collect(i - 1, turned, cs)
        inv = 1.0 / jnp.where(lowq, swap(pv), 1.0)
        mixed = pv * inv
        g = (swap(vg) * inv).astype(BF)
        gf = g.astype(F32)
        rd = jnp.sum(jnp.where(lowq, gf * mixed, 0.0), axis=1, keepdims=True)
        r1 = rd.astype(BF).astype(F32)
        r2 = (rd - r1).astype(BF).astype(F32)
        r3 = rd - r1 - r2
        gx = jnp.where(lane == 64, -r1, jnp.where(lane == 65, -r2, jnp.where(lane == 66, -r3, 0.0)))
        gx = jnp.where(lowq, gf, gx).astype(BF)
        turned = jnp.where(lowq, gf, swap(qk)).T.astype(BF)
        more = i + 1 < blocks
        if more:
            qk, vg = load(i + 1)
            qx = left(qk)
        gq, top = None, None
        for cs in chunks:
            if more:
                top = scores(i + 1, qx, cs, top)
            dp = dot(gx, vt_ref[:, cs])
            ds = (s_ref[i % 2, :, cs] * dp).astype(BF)
            d_ref[i % 2, :, cs] = ds
            part = dot(ds, kn_ref[cs, :])
            gq = part if gq is None else gq + part
        both = jnp.where(lowq, mixed, gq * SCALE).T.astype(BF)
        out_ref[2 * i, 0:128, :] = both[:, :128]
        out_ref[2 * i + 1, 0:128, :] = both[:, 128:]
    for cs in chunks:
        collect(blocks - 1, turned, cs)
    for j in range(H):
        c = slice(128 * j, 128 * j + 128)
        out_ref[j, 128:192, :] = (dk_ref[:, c] * SCALE).astype(BF)
        out_ref[j, 192:256, :] = dv_ref[:, c].astype(BF)


def attend(count, past, packed):
    return pl.pallas_call(
        attend_kernel,
        in_specs=[SMEM, SMEM, VMEM],
        out_specs=VMEM,
        out_shape=jax.ShapeDtypeStruct((H, 256, ROWS), BF),
        scratch_shapes=[
            pltpu.VMEM((KEYS, 128), BF),
            pltpu.VMEM((KEYS, 128), BF),
            pltpu.VMEM((128, KEYS), BF),
            pltpu.VMEM((128, KEYS), BF),
            pltpu.VMEM((64, KEYS), F32),
            pltpu.VMEM((64, KEYS), F32),
            pltpu.VMEM((2, QB, KEYS), F32),
            pltpu.VMEM((2, QB, KEYS), BF),
            pltpu.VMEM((2, QB, KEYS), BF),
        ],
        compiler_params=pltpu.CompilerParams(vmem_limit_bytes=24 * MIB),
        cost_estimate=pl.CostEstimate(flops=12 * CAND * KEYS * 256, bytes_accessed=3 * MIB, transcendentals=CAND * KEYS),
        name="attend",
    )(count, past, packed)


def weigh_kernel(where_ref, n0, n1, n2, n3, g0, g1, g2, g3, g4, g5, g6, g7, keep_ref, give_ref, acc_ref):
    i = pl.program_id(0)
    left = jnp.concatenate([g[0, 64:, :] for g in (g0, g1, g2, g3, g4, g5, g6, g7)], axis=1)
    right = jnp.concatenate([n[...] for n in (n0, n1, n2, n3)], axis=0)
    part = dot(left, right)

    @pl.when(i == 0)
    def _():
        acc_ref[...] = part

    @pl.when(i > 0)
    def _():
        acc_ref[...] += part

    @pl.when(i == pl.num_programs(0) - 1)
    def _():
        core = where_ref[16]
        for z in range(4):
            mine = pl.ds(pl.multiple_of((2 * z + core) * 128, 128), 128)
            other = pl.ds(pl.multiple_of((2 * z + 1 - core) * 128, 128), 128)
            keep_ref[z] = acc_ref[:, mine]
            give_ref[z] = acc_ref[:, other].astype(BF)


def weigh(where, normed, grads):
    fixed = lambda i, w: (0, 0, 0)
    return pl.pallas_call(
        weigh_kernel,
        grid_spec=pltpu.PrefetchScalarGridSpec(
            num_scalar_prefetch=1,
            grid=(2,),
            in_specs=[pl.BlockSpec((2 * ROWS, D), lambda i, w: (i, 0))] * 4
            + [pl.BlockSpec((1, 256, ROWS), lambda i, w, a=a: (w[a // 2 * 4 + 2 * i + a % 2], 0, 0)) for a in range(8)],
            out_specs=[pl.BlockSpec((4, 192, 128), fixed), pl.BlockSpec((4, 192, 128), fixed)],
            scratch_shapes=[pltpu.VMEM((192, D), F32)],
        ),
        out_shape=[jax.ShapeDtypeStruct((4, 192, 128), F32), jax.ShapeDtypeStruct((4, 192, 128), BF)],
        compiler_params=pltpu.CompilerParams(vmem_limit_bytes=24 * MIB),
        cost_estimate=SOON,
        name="weigh",
    )(where, *normed, *([grads] * 8))


def pair_kernel(where_ref, keep_ref, came_ref, own_ref, a_ref, b_ref, c_ref):
    z = where_ref[17]
    total = lambda s: keep_ref[(z + s) % 4] + came_ref[(z + s) % 4].astype(F32)
    own_ref[...] = total(0)
    a_ref[...] = total(1).astype(BF)
    b_ref[...] = total(2).astype(BF)
    c_ref[...] = total(3).astype(BF)


def pair(where, keep, came):
    return pl.pallas_call(
        pair_kernel,
        in_specs=[SMEM, VMEM, VMEM],
        out_specs=[VMEM] * 4,
        out_shape=[jax.ShapeDtypeStruct((192, 128), F32)] + [jax.ShapeDtypeStruct((192, 128), BF)] * 3,
        cost_estimate=SOON,
        compiler_params=pltpu.CompilerParams(vmem_limit_bytes=16 * MIB),
        name="pair",
    )(where, keep, came)


def line_kernel(own_ref, a_ref, b_ref, c_ref, out_ref):
    total = own_ref[...] + a_ref[...].astype(F32) + b_ref[...].astype(F32) + c_ref[...].astype(F32)
    total = jnp.concatenate([total, jnp.zeros((64, 128), F32)], axis=0)
    out_ref[...] = total.T.reshape(16, 8, 256)


def line(own, a, b, c):
    return pl.pallas_call(
        line_kernel,
        in_specs=[VMEM] * 4,
        out_specs=VMEM,
        out_shape=jax.ShapeDtypeStruct((16, 8, 256), F32),
        cost_estimate=SOON,
        compiler_params=pltpu.CompilerParams(vmem_limit_bytes=16 * MIB),
        name="line",
    )(own, a, b, c)


def finish_kernel(live_ref, x_ref, cot_ref, gain_ref, g_ref, wq_ref, wk_ref, wv_ref, y_ref, gx_ref, w_ref, acc_ref, sems):
    copies = [
        [
            pltpu.make_async_copy(w.at[pl.ds(j * WIDE, WIDE), :], w_ref.at[t, j], sems.at[t, j])
            for t, w in enumerate((wq_ref, wk_ref, wv_ref))
        ]
        for j in range(PARTS)
    ]
    for row in copies:
        for copy in row:
            copy.start()
    grad = lambda n: g_ref[:, 64 * n : 64 * n + 64, :].reshape(D, ROWS)
    x = x_ref[...].astype(F32)
    y_ref[...] = (x + grad(0).astype(F32).T).astype(BF)
    for j in range(PARTS):
        for copy in copies[j]:
            copy.wait()
        total = dot(w_ref[0, j], grad(1)) + dot(w_ref[1, j], grad(2)) + dot(w_ref[2, j], grad(3))
        acc_ref[:, WIDE * j : WIDE * j + WIDE] = total.T
    inv = inverse_rms(x)
    scaled = acc_ref[...] * gain_ref[...]
    g = cot_ref[...].astype(F32)
    g = jnp.where(rows_of(g.shape) < live_ref[0], g, 0.0)
    mean = jnp.mean(scaled * x, axis=-1, keepdims=True)
    gx_ref[...] = (g + inv * scaled - x * (inv * inv * inv * mean)).astype(BF)


def finish(live, x, cot, gain, grads, wq, wk, wv):
    return pl.pallas_call(
        finish_kernel,
        in_specs=[SMEM] + [WHOLE] * 4 + [ANY] * 3,
        out_specs=[WHOLE] * 2,
        out_shape=[jax.ShapeDtypeStruct((ROWS, D), BF)] * 2,
        scratch_shapes=[
            pltpu.VMEM((3, PARTS, WIDE, D), BF),
            pltpu.VMEM((ROWS, D), F32),
            pltpu.SemaphoreType.DMA((3, PARTS)),
        ],
        compiler_params=pltpu.CompilerParams(vmem_limit_bytes=60 * MIB),
        cost_estimate=pl.CostEstimate(flops=6 * ROWS * D * D, bytes_accessed=8 * MIB, transcendentals=0),
        name="finish",
    )(live, x, cot, gain, grads, wq, wk, wv)


def settle_kernel(place_ref, in_ref, gain_ref, w_ref, q_ref, k_ref, v_ref, gain_out_ref):
    low = lanes((8, 128)) < 64
    for p in range(H // 2):
        s = slice(128 * p, 128 * p + 128)
        a, b = in_ref[2 * p], in_ref[2 * p + 1]
        q_ref[:, s] = jnp.where(low, a[:, :128], swap(b[:, :128]))
        k_ref[:, s] = jnp.where(low, swap(a[:, :128]), b[:, :128])
        v_ref[:, s] = jnp.where(low, a[:, 128:], swap(b[:, 128:]))
    w = w_ref[...].astype(F32)
    odd = jnp.broadcast_to(place_ref[0] % 2, (8, D)) == 1
    back = 0.0
    for t, ref in enumerate((q_ref, k_ref, v_ref)):
        back = back + ref[...] * jnp.where(odd, w[16 * t + 8 : 16 * t + 16], w[16 * t : 16 * t + 8])
    back = jnp.sum(back, axis=1, keepdims=True)
    own = lanes((8, D)) == 8 * place_ref[0] + rows_of((8, D))
    gain = jnp.sum(jnp.where(own, gain_ref[...], 0.0), axis=1, keepdims=True)
    gain_out_ref[...] = jnp.broadcast_to(back / gain, (8, 128)).T[0:1, :8]


def settle(place, parts, gain, weights):
    return pl.pallas_call(
        settle_kernel,
        in_specs=[SMEM, VMEM, VMEM, VMEM],
        out_specs=[WHOLE] * 4,
        out_shape=[jax.ShapeDtypeStruct((8, D), F32)] * 3 + [jax.ShapeDtypeStruct((1, 8), F32)],
        compiler_params=pltpu.CompilerParams(vmem_limit_bytes=16 * MIB),
        name="settle",
    )(place, parts, gain, weights)


def in_plane(a, first, move):
    pairs = []
    for i in range(128):
        spot = i % 16
        if (i // 16 % 2 == 0) == first:
            spot = spot // 4 * 4 + move(spot % 4)
        else:
            spot = move(spot // 4) * 4 + spot % 4
        pairs.append((i, i // 16 * 16 + spot))
    return lax.ppermute(a, ("dp", "list"), pairs)


def along_z(a, s):
    return lax.ppermute(a, "dp", [(i, (i + 2 * s) % 8) for i in range(8)])


def other_core(a):
    return lax.ppermute(a, "dp", [(i, i ^ 1) for i in range(8)])


def body(candidates, counts, hist_keys, hist_values, hist_lengths, gain, w_query, w_key, w_value, cotangent):
    x, cot = candidates[0], cotangent[0]
    spot, part = lax.axis_index("list"), lax.axis_index("dp")
    live = counts - spot * ROWS
    gains = gain[None]
    a, i = jnp.arange(16) // 4, jnp.arange(16) % 4
    core = part % 2
    source = spot ^ jnp.where(core == 0, 4 * a + i, 4 * i + a)
    where = jnp.concatenate([source, jnp.stack([core, part // 2])]).astype(jnp.int32)
    place = (part * 16 + spot).astype(jnp.int32)[None]

    blocks = [x] + [in_plane(x, True, lambda p, s=s: p ^ s) for s in (1, 2, 3)]
    packed, own_weights = project(live, place, x, cot, hist_keys[0], hist_values[0], gains, w_query, w_key, w_value)
    packed, where, *blocks = lax.optimization_barrier((packed, where, *blocks))
    packed = lax.all_to_all(packed, "list", 0, 0, tiled=True)
    normed = gather(blocks, gains)
    normed = [normed] + [in_plane(normed, False, lambda p, s=s: p ^ s) for s in (1, 2, 3)]
    grads = attend(counts, hist_lengths, packed)
    back = lax.all_to_all(grads, "list", 0, 0, tiled=True)
    keep, give = weigh(where, normed, grads)
    own, *give = pair(where, keep, other_core(give))
    parts = line(own, *[along_z(g, s) for g, s in zip(give, (1, 2, 3))])
    parts, back = lax.optimization_barrier((parts, back))
    parts = lax.all_to_all(parts, "list", 0, 0, tiled=True)
    y, grad_x = finish(live, x, cot, gains, back, w_query, w_key, w_value)
    gq, gk, gv, ggain = settle(place, parts, gains, own_weights)
    return (y[None], grad_x[None], gq, gk, gv, ggain.reshape(8))


def solution(mesh):
    rows = P("dp", "list", None)
    weights = P(("dp", "list"), None)
    return jax.shard_map(
        body,
        mesh=mesh,
        in_specs=(rows, P("dp"), rows, rows, P("dp"), P(), P(), P(), P(), rows),
        out_specs=(rows, rows, weights, weights, weights, P(("dp", "list"))),
        check_vma=False,
    )
```

```python
import math

import jax
import jax.numpy as jnp
from jax import lax
from jax.experimental import pallas as pl
from jax.experimental.pallas import tpu as pltpu
from jax.sharding import PartitionSpec as P

D = 1024
H = 16
HEAD = 64
ROWS = 128
PAST = 16
CAND = 2048
KEYS = 2304
BLOCK = ROWS + PAST
BF = jnp.bfloat16
F32 = jnp.float32
DEAD = -1e30
SCALE = 0.125
SCALE2 = SCALE / math.log(2.0)
MIB = 1 << 20


def lanes(shape):
    return lax.broadcasted_iota(jnp.int32, shape, len(shape) - 1)


def rows_of(shape):
    return lax.broadcasted_iota(jnp.int32, shape, len(shape) - 2)


def dot(a, b):
    return jnp.dot(a, b, preferred_element_type=F32)


def swap(x):
    return pltpu.roll(x, 64, 1)


def inverse_rms(x):
    return lax.rsqrt(jnp.mean(x * x, axis=-1, keepdims=True) + 1e-05)


def norm_rows(x, gain):
    return (x * inverse_rms(x) * gain).astype(BF)


SMEM = pl.BlockSpec(memory_space=pltpu.SMEM)
VMEM = pl.BlockSpec(memory_space=pltpu.VMEM)
ANY = pl.BlockSpec(memory_space=pl.ANY)
WHOLE = pl.BlockSpec()
SOON = pl.CostEstimate(flops=1, bytes_accessed=1, transcendentals=0)


PARTS = 4
WIDE = D // PARTS


def project_kernel(live_ref, place_ref, x_ref, cot_ref, hk_ref, hv_ref, gain_ref, wq_ref, wk_ref, wv_ref, out_ref, own_ref, w_ref, sems):
    copies = [
        [
            pltpu.make_async_copy(w.at[:, pl.ds(j * WIDE, WIDE)], w_ref.at[t, j], sems.at[t, j])
            for t, w in enumerate((wq_ref, wk_ref, wv_ref))
        ]
        for j in range(PARTS)
    ]
    for row in copies:
        for copy in row:
            copy.start()
    normed = norm_rows(x_ref[...].astype(F32), gain_ref[...])
    low = lanes((ROWS, 128)) < 64
    low_h = lanes((PAST, 128)) < 64
    alive = rows_of((ROWS, 128)) < live_ref[0]
    own = pl.ds(pl.multiple_of(place_ref[0] // 2 * 16, 16), 16)
    for j in range(PARTS):
        for copy in copies[j]:
            copy.wait()
        q = dot(normed, w_ref[0, j])
        k = dot(normed, w_ref[1, j])
        v = dot(normed, w_ref[2, j])
        for t in range(3):
            own_ref[16 * t : 16 * t + 16, j * WIDE : j * WIDE + WIDE] = w_ref[t, j, own, :]
        for p in range(WIDE // 128):
            s = slice(128 * p, 128 * p + 128)
            c = slice(j * WIDE + 128 * p, j * WIDE + 128 * p + 128)
            q1, k1, v1 = q[:, s], k[:, s], v[:, s]
            g1 = jnp.where(alive, cot_ref[:, c].astype(F32), 0.0)
            hk1, hv1 = hk_ref[:, c].astype(F32), hv_ref[:, c].astype(F32)
            a = (j * WIDE + 128 * p) // HEAD
            b = a + 1
            out_ref[a, :ROWS, :128] = jnp.where(low, q1, swap(k1)).astype(BF)
            out_ref[b, :ROWS, :128] = jnp.where(low, swap(q1), k1).astype(BF)
            out_ref[a, :ROWS, 128:] = jnp.where(low, v1, swap(g1)).astype(BF)
            out_ref[b, :ROWS, 128:] = jnp.where(low, swap(v1), g1).astype(BF)
            out_ref[a, ROWS:, :128] = jnp.where(low_h, 0.0, swap(hk1)).astype(BF)
            out_ref[b, ROWS:, :128] = jnp.where(low_h, 0.0, hk1).astype(BF)
            out_ref[a, ROWS:, 128:] = jnp.where(low_h, hv1, 0.0).astype(BF)
            out_ref[b, ROWS:, 128:] = jnp.where(low_h, swap(hv1), 0.0).astype(BF)


def project(live, place, x, cot, hk, hv, gain, wq, wk, wv):
    return pl.pallas_call(
        project_kernel,
        in_specs=[SMEM] * 2 + [WHOLE] * 5 + [ANY] * 3,
        out_specs=[WHOLE] * 2,
        out_shape=[jax.ShapeDtypeStruct((H, BLOCK, 256), BF), jax.ShapeDtypeStruct((48, D), BF)],
        scratch_shapes=[pltpu.VMEM((3, PARTS, D, WIDE), BF), pltpu.SemaphoreType.DMA((3, PARTS))],
        compiler_params=pltpu.CompilerParams(vmem_limit_bytes=60 * MIB),
        cost_estimate=pl.CostEstimate(flops=60 * ROWS * D * D, bytes_accessed=8 * MIB, transcendentals=0),
        name="project",
    )(live, place, x, cot, hk, hv, gain, wq, wk, wv)


def gather_kernel(a_ref, b_ref, c_ref, d_ref, gain_ref, out_ref):
    for i, ref in enumerate((a_ref, b_ref, c_ref, d_ref)):
        out_ref[ROWS * i : ROWS * i + ROWS, :] = norm_rows(ref[...].astype(F32), gain_ref[...])


def gather(blocks, gain):
    return pl.pallas_call(
        gather_kernel,
        in_specs=[VMEM] * 5,
        out_specs=VMEM,
        out_shape=jax.ShapeDtypeStruct((4 * ROWS, D), BF),
        cost_estimate=SOON,
        compiler_params=pltpu.CompilerParams(vmem_limit_bytes=16 * MIB),
        name="gather",
    )(*blocks, gain)


QB = 256
KC = 2304


def attend_kernel(count_ref, past_ref, in_ref, out_ref, kn_ref, vx_ref, kt_ref, vt_ref, dk_ref, dv_ref, s_ref, p_ref, d_ref):
    count = count_ref[0]
    past = past_ref[0]
    low = lanes((128, 128)) < 64
    top = rows_of((64, 128)) == 0
    ones = jnp.where(rows_of((64, 128)) < 3, 1.0, 0.0).astype(BF)

    for j in range(KEYS // 128):
        if j < H:
            raw = in_ref[j, :ROWS, :]
            dead = lanes((64, 128)) + 128 * j >= count
        else:
            t = j - H
            raw = in_ref[8 * t : 8 * t + 8, ROWS:, :].reshape(128, 256)
            dead = lanes((64, 128)) + 128 * t >= past
        c = slice(128 * j, 128 * j + 128)
        kn_ref[c, :] = raw[:, :128]
        qk = raw[:, :128].astype(F32)
        vg = raw[:, 128:].astype(F32)
        vx_ref[c, :] = jnp.where(low, vg, 1.0).astype(BF)
        turned = jnp.where(low, vg, qk).T.astype(BF)
        vt_ref[0:64, c] = turned[:64, :]
        vt_ref[64:128, c] = ones
        kt_ref[0:64, c] = turned[64:, :]
        kt_ref[64:128, c] = jnp.where(top & dead, DEAD, 0.0).astype(BF)

    lane = lanes((QB, 128))
    lowq = lane < 64
    unit = jnp.where(lane == 64, 1.0, 0.0)

    blocks = CAND // QB
    chunks = [slice(c, c + KC) for c in range(0, KEYS, KC)]

    def load(i):
        rows = in_ref[2 * i : 2 * i + 2, :ROWS, :].reshape(QB, 256)
        return rows[:, :128].astype(F32), rows[:, 128:].astype(F32)

    def scores(i, qx, cs, top):
        s = dot(qx, kt_ref[:, cs])
        s_ref[i % 2, :, cs] = s
        for h in range(KC // 128):
            part = s[:, 128 * h : 128 * h + 128]
            top = part if top is None else jnp.maximum(top, part)
        return top

    def left(qk):
        return jnp.where(lowq, qk, unit).astype(BF)

    def collect(i, turned, cs):
        dk, dv = dot(turned[64:, :], d_ref[i % 2, :, cs]), dot(turned[:64, :], p_ref[i % 2, :, cs])
        dk_ref[:, cs] = dk if i == 0 else dk_ref[:, cs] + dk
        dv_ref[:, cs] = dv if i == 0 else dv_ref[:, cs] + dv

    qk, vg = load(0)
    qx, top = left(qk), None
    for cs in chunks:
        top = scores(0, qx, cs, top)
    turned = None
    for i in range(blocks):
        top = jnp.max(top, axis=1, keepdims=True)
        pv = None
        for cs in chunks:
            e = jnp.exp2((s_ref[i % 2, :, cs] - top) * SCALE2)
            s_ref[i % 2, :, cs] = e
            e = e.astype(BF)
            p_ref[i % 2, :, cs] = e
            part = dot(e, vx_ref[cs, :])
            pv = part if pv is None else pv + part
            if i > 0:
                collect(i - 1, turned, cs)
        inv = 1.0 / jnp.where(lowq, swap(pv), 1.0)
        mixed = pv * inv
        g = (swap(vg) * inv).astype(BF)
        gf = g.astype(F32)
        rd = jnp.sum(jnp.where(lowq, gf * mixed, 0.0), axis=1, keepdims=True)
        r1 = rd.astype(BF).astype(F32)
        r2 = (rd - r1).astype(BF).astype(F32)
        r3 = rd - r1 - r2
        gx = jnp.where(lane == 64, -r1, jnp.where(lane == 65, -r2, jnp.where(lane == 66, -r3, 0.0)))
        gx = jnp.where(lowq, gf, gx).astype(BF)
        turned = jnp.where(lowq, gf, swap(qk)).T.astype(BF)
        more = i + 1 < blocks
        if more:
            qk, vg = load(i + 1)
            qx = left(qk)
        gq, top = None, None
        for cs in chunks:
            if more:
                top = scores(i + 1, qx, cs, top)
            dp = dot(gx, vt_ref[:, cs])
            ds = (s_ref[i % 2, :, cs] * dp).astype(BF)
            d_ref[i % 2, :, cs] = ds
            part = dot(ds, kn_ref[cs, :])
            gq = part if gq is None else gq + part
        both = jnp.where(lowq, mixed, gq * SCALE).T.astype(BF)
        out_ref[2 * i, 0:128, :] = both[:, :128]
        out_ref[2 * i + 1, 0:128, :] = both[:, 128:]
    for cs in chunks:
        collect(blocks - 1, turned, cs)
    for j in range(H):
        c = slice(128 * j, 128 * j + 128)
        out_ref[j, 128:192, :] = (dk_ref[:, c] * SCALE).astype(BF)
        out_ref[j, 192:256, :] = dv_ref[:, c].astype(BF)


def attend(count, past, packed):
    return pl.pallas_call(
        attend_kernel,
        in_specs=[SMEM, SMEM, VMEM],
        out_specs=VMEM,
        out_shape=jax.ShapeDtypeStruct((H, 256, ROWS), BF),
        scratch_shapes=[
            pltpu.VMEM((KEYS, 128), BF),
            pltpu.VMEM((KEYS, 128), BF),
            pltpu.VMEM((128, KEYS), BF),
            pltpu.VMEM((128, KEYS), BF),
            pltpu.VMEM((64, KEYS), F32),
            pltpu.VMEM((64, KEYS), F32),
            pltpu.VMEM((2, QB, KEYS), F32),
            pltpu.VMEM((2, QB, KEYS), BF),
            pltpu.VMEM((2, QB, KEYS), BF),
        ],
        compiler_params=pltpu.CompilerParams(vmem_limit_bytes=24 * MIB),
        cost_estimate=pl.CostEstimate(flops=12 * CAND * KEYS * 256, bytes_accessed=3 * MIB, transcendentals=CAND * KEYS),
        name="attend",
    )(count, past, packed)


def weigh_kernel(where_ref, n0, n1, n2, n3, g0, g1, g2, g3, g4, g5, g6, g7, keep_ref, give_ref, acc_ref):
    i = pl.program_id(0)
    left = jnp.concatenate([g[0, 64:, :] for g in (g0, g1, g2, g3, g4, g5, g6, g7)], axis=1)
    right = jnp.concatenate([n[...] for n in (n0, n1, n2, n3)], axis=0)
    part = dot(left, right)

    @pl.when(i == 0)
    def _():
        acc_ref[...] = part

    @pl.when(i > 0)
    def _():
        acc_ref[...] += part

    @pl.when(i == pl.num_programs(0) - 1)
    def _():
        core = where_ref[16]
        for z in range(4):
            mine = pl.ds(pl.multiple_of((2 * z + core) * 128, 128), 128)
            other = pl.ds(pl.multiple_of((2 * z + 1 - core) * 128, 128), 128)
            keep_ref[z] = acc_ref[:, mine]
            give_ref[z] = acc_ref[:, other].astype(BF)


def weigh(where, normed, grads):
    fixed = lambda i, w: (0, 0, 0)
    return pl.pallas_call(
        weigh_kernel,
        grid_spec=pltpu.PrefetchScalarGridSpec(
            num_scalar_prefetch=1,
            grid=(2,),
            in_specs=[pl.BlockSpec((2 * ROWS, D), lambda i, w: (i, 0))] * 4
            + [pl.BlockSpec((1, 256, ROWS), lambda i, w, a=a: (w[a // 2 * 4 + 2 * i + a % 2], 0, 0)) for a in range(8)],
            out_specs=[pl.BlockSpec((4, 192, 128), fixed), pl.BlockSpec((4, 192, 128), fixed)],
            scratch_shapes=[pltpu.VMEM((192, D), F32)],
        ),
        out_shape=[jax.ShapeDtypeStruct((4, 192, 128), F32), jax.ShapeDtypeStruct((4, 192, 128), BF)],
        compiler_params=pltpu.CompilerParams(vmem_limit_bytes=24 * MIB),
        cost_estimate=SOON,
        name="weigh",
    )(where, *normed, *([grads] * 8))


def pair_kernel(where_ref, keep_ref, came_ref, own_ref, a_ref, b_ref, c_ref):
    z = where_ref[17]
    total = lambda s: keep_ref[(z + s) % 4] + came_ref[(z + s) % 4].astype(F32)
    own_ref[...] = total(0)
    a_ref[...] = total(1).astype(BF)
    b_ref[...] = total(2).astype(BF)
    c_ref[...] = total(3).astype(BF)


def pair(where, keep, came):
    return pl.pallas_call(
        pair_kernel,
        in_specs=[SMEM, VMEM, VMEM],
        out_specs=[VMEM] * 4,
        out_shape=[jax.ShapeDtypeStruct((192, 128), F32)] + [jax.ShapeDtypeStruct((192, 128), BF)] * 3,
        cost_estimate=SOON,
        compiler_params=pltpu.CompilerParams(vmem_limit_bytes=16 * MIB),
        name="pair",
    )(where, keep, came)


def line_kernel(own_ref, a_ref, b_ref, c_ref, out_ref):
    total = own_ref[...] + a_ref[...].astype(F32) + b_ref[...].astype(F32) + c_ref[...].astype(F32)
    total = jnp.concatenate([total, jnp.zeros((64, 128), F32)], axis=0)
    total = total.T.reshape(16, 8, 256)
    out_ref[...] = jnp.concatenate([total[:, :, :128], total[:, :, 128:]], axis=1).astype(BF)


def line(own, a, b, c):
    return pl.pallas_call(
        line_kernel,
        in_specs=[VMEM] * 4,
        out_specs=VMEM,
        out_shape=jax.ShapeDtypeStruct((16, 16, 128), BF),
        cost_estimate=SOON,
        compiler_params=pltpu.CompilerParams(vmem_limit_bytes=16 * MIB),
        name="line",
    )(own, a, b, c)


def finish_kernel(live_ref, x_ref, cot_ref, gain_ref, g_ref, wq_ref, wk_ref, wv_ref, y_ref, gx_ref, w_ref, acc_ref, sems):
    copies = [
        [
            pltpu.make_async_copy(w.at[pl.ds(j * WIDE, WIDE), :], w_ref.at[t, j], sems.at[t, j])
            for t, w in enumerate((wq_ref, wk_ref, wv_ref))
        ]
        for j in range(PARTS)
    ]
    for row in copies:
        for copy in row:
            copy.start()
    grad = lambda n: g_ref[:, 64 * n : 64 * n + 64, :].reshape(D, ROWS)
    x = x_ref[...].astype(F32)
    y_ref[...] = (x + grad(0).astype(F32).T).astype(BF)
    for j in range(PARTS):
        for copy in copies[j]:
            copy.wait()
        total = dot(w_ref[0, j], grad(1)) + dot(w_ref[1, j], grad(2)) + dot(w_ref[2, j], grad(3))
        acc_ref[:, WIDE * j : WIDE * j + WIDE] = total.T
    inv = inverse_rms(x)
    scaled = acc_ref[...] * gain_ref[...]
    g = cot_ref[...].astype(F32)
    g = jnp.where(rows_of(g.shape) < live_ref[0], g, 0.0)
    mean = jnp.mean(scaled * x, axis=-1, keepdims=True)
    gx_ref[...] = (g + inv * scaled - x * (inv * inv * inv * mean)).astype(BF)


def finish(live, x, cot, gain, grads, wq, wk, wv):
    return pl.pallas_call(
        finish_kernel,
        in_specs=[SMEM] + [WHOLE] * 4 + [ANY] * 3,
        out_specs=[WHOLE] * 2,
        out_shape=[jax.ShapeDtypeStruct((ROWS, D), BF)] * 2,
        scratch_shapes=[
            pltpu.VMEM((3, PARTS, WIDE, D), BF),
            pltpu.VMEM((ROWS, D), F32),
            pltpu.SemaphoreType.DMA((3, PARTS)),
        ],
        compiler_params=pltpu.CompilerParams(vmem_limit_bytes=60 * MIB),
        cost_estimate=pl.CostEstimate(flops=6 * ROWS * D * D, bytes_accessed=8 * MIB, transcendentals=0),
        name="finish",
    )(live, x, cot, gain, grads, wq, wk, wv)


def settle_kernel(place_ref, in_ref, gain_ref, w_ref, q_ref, k_ref, v_ref, gain_out_ref):
    low = lanes((8, 128)) < 64
    for p in range(H // 2):
        s = slice(128 * p, 128 * p + 128)
        a, b = in_ref[2 * p].astype(F32), in_ref[2 * p + 1].astype(F32)
        q_ref[:, s] = jnp.where(low, a[:8], swap(b[:8]))
        k_ref[:, s] = jnp.where(low, swap(a[:8]), b[:8])
        v_ref[:, s] = jnp.where(low, a[8:], swap(b[8:]))
    w = w_ref[...].astype(F32)
    odd = jnp.broadcast_to(place_ref[0] % 2, (8, D)) == 1
    back = 0.0
    for t, ref in enumerate((q_ref, k_ref, v_ref)):
        back = back + ref[...] * jnp.where(odd, w[16 * t + 8 : 16 * t + 16], w[16 * t : 16 * t + 8])
    back = jnp.sum(back, axis=1, keepdims=True)
    own = lanes((8, D)) == 8 * place_ref[0] + rows_of((8, D))
    gain = jnp.sum(jnp.where(own, gain_ref[...], 0.0), axis=1, keepdims=True)
    gain_out_ref[...] = jnp.broadcast_to(back / gain, (8, 128)).T[0:1, :8]


def settle(place, parts, gain, weights):
    return pl.pallas_call(
        settle_kernel,
        in_specs=[SMEM, VMEM, VMEM, VMEM],
        out_specs=[WHOLE] * 4,
        out_shape=[jax.ShapeDtypeStruct((8, D), F32)] * 3 + [jax.ShapeDtypeStruct((1, 8), F32)],
        compiler_params=pltpu.CompilerParams(vmem_limit_bytes=16 * MIB),
        name="settle",
    )(place, parts, gain, weights)


def in_plane(a, first, move):
    pairs = []
    for i in range(128):
        spot = i % 16
        if (i // 16 % 2 == 0) == first:
            spot = spot // 4 * 4 + move(spot % 4)
        else:
            spot = move(spot // 4) * 4 + spot % 4
        pairs.append((i, i // 16 * 16 + spot))
    return lax.ppermute(a, ("dp", "list"), pairs)


def along_z(a, s):
    return lax.ppermute(a, "dp", [(i, (i + 2 * s) % 8) for i in range(8)])


def other_core(a):
    return lax.ppermute(a, "dp", [(i, i ^ 1) for i in range(8)])


def body(candidates, counts, hist_keys, hist_values, hist_lengths, gain, w_query, w_key, w_value, cotangent):
    x, cot = candidates[0], cotangent[0]
    spot, part = lax.axis_index("list"), lax.axis_index("dp")
    live = counts - spot * ROWS
    gains = gain[None]
    a, i = jnp.arange(16) // 4, jnp.arange(16) % 4
    core = part % 2
    source = spot ^ jnp.where(core == 0, 4 * a + i, 4 * i + a)
    where = jnp.concatenate([source, jnp.stack([core, part // 2])]).astype(jnp.int32)
    place = (part * 16 + spot).astype(jnp.int32)[None]

    blocks = [x] + [in_plane(x, True, lambda p, s=s: p ^ s) for s in (1, 2, 3)]
    packed, own_weights = project(live, place, x, cot, hist_keys[0], hist_values[0], gains, w_query, w_key, w_value)
    packed, where, *blocks = lax.optimization_barrier((packed, where, *blocks))
    packed = lax.all_to_all(packed, "list", 0, 0, tiled=True)
    normed = gather(blocks, gains)
    normed = [normed] + [in_plane(normed, False, lambda p, s=s: p ^ s) for s in (1, 2, 3)]
    grads = attend(counts, hist_lengths, packed)
    back = lax.all_to_all(grads, "list", 0, 0, tiled=True)
    keep, give = weigh(where, normed, grads)
    own, *give = pair(where, keep, other_core(give))
    parts = line(own, *[along_z(g, s) for g, s in zip(give, (1, 2, 3))])
    parts, back = lax.optimization_barrier((parts, back))
    parts = lax.all_to_all(parts, "list", 0, 0, tiled=True)
    y, grad_x = finish(live, x, cot, gains, back, w_query, w_key, w_value)
    gq, gk, gv, ggain = settle(place, parts, gains, own_weights)
    return (y[None], grad_x[None], gq, gk, gv, ggain.reshape(8))


def solution(mesh):
    rows = P("dp", "list", None)
    weights = P(("dp", "list"), None)
    return jax.shard_map(
        body,
        mesh=mesh,
        in_specs=(rows, P("dp"), rows, rows, P("dp"), P(), P(), P(), P(), rows),
        out_specs=(rows, rows, weights, weights, weights, P(("dp", "list"))),
        check_vma=False,
    )
```
